32 devices in a mesh: ctx: 4 (over z), tp: 4 (over y, x), dp: 2 (over core).
Axes of the slice: x: 2, y: 2, z: 4, core: 2. Of those that a mesh axis runs over, the one named last changes fastest.
Arguments:
- out_grad: bfloat16 [2, 512, 4096], P('dp', ('ctx', 'tp')), may hold values from -6 to 6
- gate_in: bfloat16 [2, 4096, 512], P('dp', 'tp', 'ctx'), may hold values from -6 to 6
- conv_in: bfloat16 [2, 4096, 512], P('dp', 'tp', 'ctx'), may hold values from -6 to 6
- filter_raw: float32 [4096, 512], P(('tp', 'ctx')), may hold values from -6 to 6
- out_weight: bfloat16 [4096, 4096], P('tp'), may hold values from -0.09375 to 0.09375
Outputs:
- gate_grad_out: bfloat16 [2, 4096, 512], P('dp', 'tp', 'ctx')
- conv_grad_out: bfloat16 [2, 4096, 512], P('dp', 'tp', 'ctx')
- filter_grad_out: float32 [4096, 512], P(('tp', 'ctx', 'dp'))
The draws below stay inside these ranges and needn't reach their ends.
All inputs are finite; a program needn't handle non-finite values.
Results may differ from the reference program's by a relative error of at most 0.0049.
Values may be sent and summed in bfloat16 or wider, within the bound.
No kernel may reach another device: no remote copies, remote signals or barrier semaphores. Data moves between devices by JAX's collectives and lax.ppermute only.
A program may use at most 64 MiB of HBM per device.

```python
import jax
import jax.numpy as jnp
from jax import lax

D = 4096
LEN = 512
SEQS = 2


def steps_of(rng, shape, split, smallest, high):
    loudness = 1.0
    for axis_at, parts in split:
        heights = jax.random.uniform(jax.random.fold_in(jax.random.fold_in(rng, 6), axis_at), (parts,), jnp.float32, smallest / len(split), high / len(split))
        loudness = loudness * jnp.repeat(jnp.exp(heights), shape[axis_at] // parts).reshape((-1,) + (1,) * (len(shape) - 1 - axis_at))
    return loudness


def noise(stream_key, shape, spread, limit, split=(), kind=jnp.bfloat16):
    entries = spread * jax.random.normal(stream_key, shape, jnp.float32)
    if split:
        entries = entries * steps_of(stream_key, shape, split, -0.22, 0.18)
    return jnp.clip(entries, -limit, limit).astype(kind)


def setup_inputs(seed: int = 0) -> dict:
    splits = jax.random.split(jax.random.key(seed), 6)
    return {
        "out_grad": noise(splits[0], (SEQS, LEN, D), 1.0, 6.0, ((0, 2), (1, 16))),
        "gate_in": noise(splits[1], (SEQS, D, LEN), 1.0, 6.0, ((0, 2), (1, 4), (2, 4))),
        "conv_in": noise(splits[2], (SEQS, D, LEN), 1.0, 6.0, ((0, 2), (1, 4), (2, 4))),
        "filter_raw": noise(splits[3], (D, LEN), 1.0, 6.0, ((0, 16),), jnp.float32),
        "out_weight": noise(splits[4], (D, D), D ** -0.5, 0.09375, ((0, 4),)),
    }


def reference(out_grad, gate_in, conv_in, filter_raw, out_weight):
    total_len = 2 * LEN
    root_len = jnp.sqrt(jnp.float32(LEN))
    filt = filter_raw / root_len
    spec_filt = jnp.fft.rfft(filt, n=total_len, axis=-1)

    def one_seq(total, items):
        grad_seq, gate_seq, conv_seq = items
        unit_grad = jnp.dot(out_weight, jnp.transpose(grad_seq), preferred_element_type=jnp.float32)
        gate_grad = (unit_grad * gate_seq.astype(jnp.float32)).astype(jnp.bfloat16)
        spec_conv = jnp.fft.rfft(conv_seq.astype(jnp.float32), n=total_len, axis=-1)
        spec_gate = jnp.fft.rfft(gate_grad.astype(jnp.float32), n=total_len, axis=-1)
        conv_out = jnp.fft.irfft(spec_filt * spec_conv, n=total_len, axis=-1)[:, :LEN].astype(jnp.bfloat16)
        conv_grad = jnp.fft.irfft(jnp.conj(spec_filt) * spec_gate, n=total_len, axis=-1)[:, :LEN].astype(jnp.bfloat16)
        filt_term = jnp.fft.irfft(spec_gate * jnp.conj(spec_conv), n=total_len, axis=-1)[:, :LEN] / root_len
        gate_out = (unit_grad * conv_out.astype(jnp.float32)).astype(jnp.bfloat16)
        return (total + filt_term, (gate_out, conv_grad))
    total, (gate_grad_out, conv_grad_out) = lax.scan(one_seq, jnp.zeros((D, LEN), jnp.float32), (out_grad, gate_in, conv_in))
    return (gate_grad_out, conv_grad_out, total)
```

```python
import functools
import math

import jax
import jax.numpy as jnp
import ml_dtypes
import numpy as np
from jax import lax
from jax.experimental import pallas as pl
from jax.experimental.pallas import tpu as pltpu
from jax.sharding import PartitionSpec as P


def wave_table(rows, cols, length, sign):
    product = (
        jnp.arange(rows, dtype=jnp.int32)[:, None]
        * jnp.arange(cols, dtype=jnp.int32)[None, :]
        % length
    )
    angle = product.astype(jnp.float32) * (2.0 * math.pi / length)
    return (jnp.cos(angle), sign * jnp.sin(angle))


def mix_einsum(form, left, right):
    return jnp.einsum(form, left, right, precision=lax.Precision.HIGHEST)


def forward_spectrum(signal):
    chans, length = signal.shape
    total_len = 2 * length
    bits = total_len.bit_length() - 1
    outer_len = 2 ** (bits // 2)
    inner_len = total_len // outer_len
    half_outer = outer_len // 2
    folded = signal.reshape(chans, half_outer, inner_len)
    first_re, first_im = wave_table(outer_len, half_outer, outer_len, -1.0)
    mid_re = mix_einsum("kn,cna->cka", first_re, folded)
    mid_im = mix_einsum("kn,cna->cka", first_im, folded)
    twist_re, twist_im = wave_table(outer_len, inner_len, total_len, -1.0)
    rot_re = mid_re * twist_re - mid_im * twist_im
    rot_im = mid_re * twist_im + mid_im * twist_re
    last_re, last_im = wave_table(inner_len, inner_len, inner_len, -1.0)
    out_re = mix_einsum("cka,aj->ckj", rot_re, last_re) - mix_einsum("cka,aj->ckj", rot_im, last_im)
    out_im = mix_einsum("cka,aj->ckj", rot_re, last_im) + mix_einsum("cka,aj->ckj", rot_im, last_re)
    return (out_re, out_im)


def inverse_signal(spec_re, spec_im):
    chans, outer_len, inner_len = spec_re.shape
    total_len = outer_len * inner_len
    last_re, last_im = wave_table(inner_len, inner_len, inner_len, 1.0)
    mid_re = mix_einsum("ckj,ja->cka", spec_re, last_re) - mix_einsum(
        "ckj,ja->cka", spec_im, last_im
    )
    mid_im = mix_einsum("ckj,ja->cka", spec_re, last_im) + mix_einsum(
        "ckj,ja->cka", spec_im, last_re
    )
    twist_re, twist_im = wave_table(outer_len, inner_len, total_len, 1.0)
    rot_re = mid_re * twist_re - mid_im * twist_im
    rot_im = mid_re * twist_im + mid_im * twist_re
    first_re, first_im = wave_table(outer_len // 2, outer_len, outer_len, 1.0)
    signal = mix_einsum("nk,cka->cna", first_re, rot_re) - mix_einsum(
        "nk,cka->cna", first_im, rot_im
    )
    return signal.reshape(chans, -1) / total_len


def two_level_on_device(out_grad, gate_in, conv_in, filter_raw, out_weight):
    grad_rows = out_grad[0]
    gate_local = gate_in[0]
    conv_local = conv_in[0]
    unit_grad = lax.dot_general(
        out_weight,
        lax.all_gather(grad_rows, "tp", axis=0, tiled=True),
        (((1,), (1,)), ((), ())),
        preferred_element_type=jnp.float32,
    )
    gate_grad = (unit_grad * gate_local.astype(jnp.float32)).astype(jnp.bfloat16)
    gate_chan, conv_chan = (
        lax.all_to_all(gate_grad, "ctx", split_axis=0, concat_axis=1, tiled=True),
        lax.all_to_all(conv_local, "ctx", split_axis=0, concat_axis=1, tiled=True),
    )
    length = filter_raw.shape[1]
    norm_scale = 1.0 / math.sqrt(length)
    filt_re, filt_im = forward_spectrum(filter_raw * norm_scale)
    conv_re, conv_im = forward_spectrum(conv_chan.astype(jnp.float32))
    gate_re, gate_im = forward_spectrum(gate_chan.astype(jnp.float32))
    conv_out = inverse_signal(
        filt_re * conv_re - filt_im * conv_im, filt_re * conv_im + filt_im * conv_re
    ).astype(jnp.bfloat16)
    conv_grad = inverse_signal(
        filt_re * gate_re + filt_im * gate_im, filt_re * gate_im - filt_im * gate_re
    ).astype(jnp.bfloat16)
    cross_re = gate_re * conv_re + gate_im * conv_im
    cross_im = gate_im * conv_re - gate_re * conv_im
    back_out, back_grad = (
        lax.all_to_all(conv_out, "ctx", split_axis=1, concat_axis=0, tiled=True),
        lax.all_to_all(conv_grad, "ctx", split_axis=1, concat_axis=0, tiled=True),
    )
    gate_out = (unit_grad * back_out.astype(jnp.float32)).astype(jnp.bfloat16)
    summed_re, summed_im = (
        lax.psum_scatter(cross_re * norm_scale, "dp", scatter_dimension=0, tiled=True),
        lax.psum_scatter(cross_im * norm_scale, "dp", scatter_dimension=0, tiled=True),
    )
    filter_grad = inverse_signal(summed_re, summed_im)
    return (gate_out[None], back_grad[None], filter_grad)


TABLE_LIMIT_BYTES = 4 * 2**20
VMEM_BYTES = 24 * 2**20


def split_high_low(values):
    high = values.astype(ml_dtypes.bfloat16)
    low = (values - high.astype(np.float64)).astype(ml_dtypes.bfloat16)
    return high, low


@functools.lru_cache(maxsize=None)
def dense_tables(length):
    total = 2 * length
    time = np.arange(length)[:, None]
    freq = np.arange(length)[None, :]
    angle = (time * freq % total) * (2.0 * np.pi / total)
    even_odd = 1.0 - 2.0 * (np.arange(length) % 2)
    real, imag = np.cos(angle), -np.sin(angle)
    imag[:, 0] = even_odd
    weight = np.full((length, 1), 2.0 / total)
    weight[0] = 1.0 / total
    forward = np.concatenate([real, imag], axis=1)
    inverse = np.concatenate([real.T * weight, imag.T * weight], axis=0)
    return split_high_low(forward) + split_high_low(inverse)


def mm(left, right):
    return jnp.dot(left, right, preferred_element_type=jnp.float32)


def mm_nt(left, right):
    return lax.dot_general(left, right, (((1,), (1,)), ((), ())), preferred_element_type=jnp.float32)


def halves(values):
    high = values.astype(jnp.bfloat16)
    return high, (values - high.astype(jnp.float32)).astype(jnp.bfloat16)


def spectrum_product(left, right, conj_left):
    length = left.shape[1] // 2
    lr, li = left[:, :length], left[:, length:]
    rr, ri = right[:, :length], right[:, length:]
    ends = lax.broadcasted_iota(jnp.int32, lr.shape, 1) == 0
    both = li * ri
    if conj_left:
        real = lr * rr + jnp.where(ends, 0.0, both)
        imag = jnp.where(ends, both, lr * ri - li * rr)
    else:
        real = lr * rr - jnp.where(ends, 0.0, both)
        imag = jnp.where(ends, both, lr * ri + li * rr)
    return jnp.concatenate([real, imag], axis=1)


def inverse_dense(spec, inv_hi, inv_lo):
    high, low = halves(spec)
    return mm(high, inv_hi[...]) + mm(low, inv_hi[...]) + mm(high, inv_lo[...])


def place(index, size):
    return pl.ds(pl.multiple_of(index * size, size), size)


def offsets(parts):
    return [0, *reversed(range(1, parts))]


def gather_tokens(pieces, whole, here):
    step = pieces[0].shape[1]
    for k, piece in zip(offsets(len(pieces)), pieces):
        whole[:, place(here ^ k, step)] = piece[...]


def scatter_tokens(whole, pieces, here):
    step = pieces[0].shape[1]
    for k, piece in zip(offsets(len(pieces)), pieces):
        piece[...] = whole[:, place(here ^ k, step)]


def blocks_kernel(source, *refs):
    out, sems = refs[:-1], refs[-1]
    here = lax.axis_index("ctx")
    rows = out[0].shape[0]
    copies = [
        pltpu.make_async_copy(source.at[place(here ^ k, rows), :], ref, sems.at[k])
        for k, ref in zip(offsets(len(out)), out)
    ]
    for copy in copies:
        copy.start()
    for copy in copies:
        copy.wait()


def filt_kernel(scale, filt, fwd_hi, fwd_lo, spec_filt):
    high, low = halves(filt[...] * scale)
    spec_filt[...] = mm(high, fwd_hi[...]) + mm(low, fwd_hi[...]) + mm(high, fwd_lo[...])


def spectrum_of(signal, fwd_hi, fwd_lo):
    return mm(signal, fwd_hi[...]) + mm(signal, fwd_lo[...])


def pair_rows(rows, mine):
    at = lax.axis_index("dp")
    return place(at if mine else 1 - at, rows)


def conv_kernel(parts, *refs):
    conv = refs[:parts]
    spec_filt, fwd_hi, fwd_lo, inv_hi, inv_lo = refs[parts : parts + 5]
    out = refs[parts + 5 : 2 * parts + 5]
    spec_own, send, spec_conv, whole = refs[2 * parts + 5 :]
    here = lax.axis_index("ctx")
    gather_tokens(conv, whole, here)
    rows = send.shape[0]
    send[...] = whole[pair_rows(rows, False), :]
    spec_conv[...] = spectrum_of(whole[...], fwd_hi, fwd_lo)
    product = spectrum_product(spec_filt[...], spec_conv[...], False)
    spec_own[...] = spec_conv[pair_rows(rows, True), :]
    whole[...] = inverse_dense(product, inv_hi, inv_lo).astype(jnp.bfloat16)
    scatter_tokens(whole, out, here)


def unit_kernel(parts, pieces, after, weight, gate, *refs):
    grads = refs[:pieces]
    unit = refs[pieces]
    out = refs[pieces + 1 : pieces + 1 + parts]
    rows_all = refs[pieces + 1 + parts]
    here, block = lax.axis_index("ctx"), lax.axis_index("tp")
    rows = grads[0].shape[0]
    half = rows_all.shape[1] // 2
    for k, ref in enumerate(grads[:3]):
        rows_all[place(block ^ k, rows), :] = ref[...]
    rows_all[place(block ^ 3, rows), :half] = grads[3][...]
    rows_all[place(block ^ 3, rows), half:] = grads[4][...]
    rows = out[0].shape[0]
    unit[...] = mm_nt(weight[...], rows_all[...])
    for k, ref in zip(offsets(parts), out):
        at = place(here ^ k, rows)
        ref[...] = (unit[at, :] * gate[at, :].astype(jnp.float32)).astype(jnp.bfloat16)


def grad_kernel(parts, *refs):
    gate = refs[:parts]
    spec_filt, fwd_hi, fwd_lo, inv_hi, inv_lo = refs[parts : parts + 5]
    out = refs[parts + 5 : 2 * parts + 5]
    spec_own, *send, spec_gate, whole = refs[2 * parts + 5 :]
    here = lax.axis_index("ctx")
    gather_tokens(gate, whole, here)
    rows = spec_own.shape[0]
    for i, ref in enumerate(send):
        at = pair_rows(rows, False).start + i * ref.shape[0]
        ref[...] = whole[pl.ds(pl.multiple_of(at, ref.shape[0]), ref.shape[0]), :]
    spec_gate[...] = spectrum_of(whole[...], fwd_hi, fwd_lo)
    product = spectrum_product(spec_filt[...], spec_gate[...], True)
    spec_own[...] = spec_gate[pair_rows(rows, True), :]
    whole[...] = inverse_dense(product, inv_hi, inv_lo).astype(jnp.bfloat16)
    scatter_tokens(whole, out, here)


def filter_kernel(parts, scale, spec_conv, spec_gate, conv_peer, gate_low, gate_high, *refs):
    fwd_hi, fwd_lo, inv_hi, inv_lo, unit = refs[:5]
    back = refs[5 : 5 + parts]
    filter_grad, out = refs[5 + parts :]
    here = lax.axis_index("ctx")
    rows = back[0].shape[0]
    for k, ref in zip(offsets(parts), back):
        at = place(here ^ k, rows)
        out[at, :] = (unit[at, :] * ref[...].astype(jnp.float32)).astype(jnp.bfloat16)
    conv_peer = spectrum_of(conv_peer[...], fwd_hi, fwd_lo)
    gate_peer = jnp.concatenate([gate_low[...], gate_high[...]], axis=0)
    gate_peer = spectrum_of(gate_peer, fwd_hi, fwd_lo)
    product = spectrum_product(spec_conv[...], spec_gate[...], True)
    product = product + spectrum_product(conv_peer, gate_peer, True)
    filter_grad[...] = inverse_dense(product, inv_hi, inv_lo) * scale


def last_kernel(parts, after, *refs):
    back, out = refs[:parts], refs[parts]
    here = lax.axis_index("ctx")
    rows = back[0].shape[0]
    for k, ref in zip(offsets(parts), back):
        out[place(here ^ k, rows), :] = ref[...]


def call(kernel, outs, args, scratch=(), far=0, cost=1.0):
    vmem = pl.BlockSpec(memory_space=pltpu.VMEM)
    hbm = pl.BlockSpec(memory_space=pltpu.HBM)
    held = [pltpu.with_memory_space_constraint(a, pltpu.HBM) for a in args[:far]]
    return pl.pallas_call(
        kernel,
        out_shape=outs,
        in_specs=[hbm] * far + [vmem] * (len(args) - far),
        out_specs=jax.tree.map(lambda _: vmem, outs),
        scratch_shapes=list(scratch),
        cost_estimate=pl.CostEstimate(
            flops=int(cost * 1e9), bytes_accessed=int(cost * 1e6), transcendentals=0
        ),
        compiler_params=pltpu.CompilerParams(vmem_limit_bytes=VMEM_BYTES),
    )(*held, *args[far:])


def dense_on_device(parts, groups, out_grad, gate_in, conv_in, filter_raw, out_weight):
    f32, bf16 = jnp.float32, jnp.bfloat16
    grad_rows, gate_local, conv_local = out_grad[0], gate_in[0], conv_in[0]
    chans, length = filter_raw.shape
    channels, tokens = conv_local.shape
    width = grad_rows.shape[1]
    scale = 1.0 / math.sqrt(length)
    tables = [jnp.asarray(t) for t in dense_tables(length)]
    shape = jax.ShapeDtypeStruct
    def swap(value, axis, size, k):
        return lax.ppermute(value, axis, [(i, i ^ k) for i in range(size)])

    def exchange(pieces):
        order = offsets(parts)[: len(pieces)]
        return [swap(p, "ctx", parts, k) if k else p for k, p in zip(order, pieces)]

    grad_1 = swap(grad_rows, "tp", groups, 1)
    grad_2 = swap(grad_rows, "tp", groups, 2)
    blocks = call(
        blocks_kernel,
        [shape((chans, tokens), bf16)] * parts,
        [conv_local],
        [pltpu.SemaphoreType.DMA((parts,))],
        far=1,
        cost=10.0,
    )
    conv_pieces = exchange(blocks)
    grad_3a = swap(grad_1[:, : width // 2], "tp", groups, 2)
    grad_3b = swap(grad_2[:, width // 2 :], "tp", groups, 1)

    piece = shape((chans, tokens), bf16)
    spectrum = shape((chans, 2 * length), f32)
    whole = pltpu.VMEM((chans, length), bf16)
    spec_filt = call(
        functools.partial(filt_kernel, scale), spectrum, [filter_raw, *tables[:2]], cost=2.0
    )
    half, half_spectrum = (chans // 2, length), shape((chans // 2, 2 * length), f32)
    work = [pltpu.VMEM(spectrum.shape, f32), whole]
    *conv_out, spec_conv, conv_send = call(
        functools.partial(conv_kernel, parts),
        [piece] * parts + [half_spectrum, shape(half, bf16)],
        [*conv_pieces, spec_filt, *tables],
        work,
        cost=2.0,
    )
    conv_back = exchange(conv_out)

    unit, *gate_pieces = call(
        functools.partial(unit_kernel, parts, 5),
        [shape((channels, tokens), f32)] + [piece] * parts,
        [conv_out[0], out_weight, gate_local, grad_rows, grad_1, grad_2, grad_3a, grad_3b],
        [pltpu.VMEM((groups * grad_rows.shape[0], width), bf16)],
    )
    gate_chan = exchange(gate_pieces)
    quarter = shape((half[0] // 2, length), bf16)
    *conv_grad, spec_gate, send_low, send_high = call(
        functools.partial(grad_kernel, parts),
        [piece] * parts + [half_spectrum, quarter, quarter],
        [*gate_chan, spec_filt, *tables],
        work,
    )
    grad_back = exchange(conv_grad)
    peer = [swap(a, "dp", 2, 1) for a in (conv_send, send_low, send_high)]
    local = shape((channels, tokens), bf16)
    filter_grad, gate_out = call(
        functools.partial(filter_kernel, parts, scale),
        [shape(half, f32), local],
        [spec_conv, spec_gate, *peer, *tables, unit, *conv_back],
        cost=2.0,
    )
    conv_grad_out = call(
        functools.partial(last_kernel, parts), local, [filter_grad, *grad_back], far=1
    )
    return (gate_out[None], conv_grad_out[None], filter_grad)


def solution(mesh):
    placed = (
        P("dp", ("ctx", "tp"), None),
        P("dp", "tp", "ctx"),
        P("dp", "tp", "ctx"),
        P(("tp", "ctx"), None),
        P("tp", None),
    )
    parts, groups, pair = mesh.shape["ctx"], mesh.shape["tp"], mesh.shape["dp"]

    def on_device(out_grad, gate_in, conv_in, filter_raw, out_weight):
        args = (out_grad, gate_in, conv_in, filter_raw, out_weight)
        table = 4 * filter_raw.shape[1] ** 2 * jnp.dtype(jnp.bfloat16).itemsize
        one_sequence = out_grad.shape[0] == 1
        power = parts & (parts - 1) == 0
        if one_sequence and power and parts > 1 and groups == 4 and pair == 2 and table <= TABLE_LIMIT_BYTES:
            return dense_on_device(parts, groups, *args)
        return two_level_on_device(*args)

    return jax.shard_map(
        on_device,
        mesh=mesh,
        in_specs=placed,
        out_specs=(P("dp", "tp", "ctx"), P("dp", "tp", "ctx"), P(("tp", "ctx", "dp"), None)),
        check_vma=False,
    )
```

```python
import functools
import math

import jax
import jax.numpy as jnp
import ml_dtypes
import numpy as np
from jax import lax
from jax.experimental import pallas as pl
from jax.experimental.pallas import tpu as pltpu
from jax.sharding import PartitionSpec as P


def wave_table(rows, cols, length, sign):
    product = (
        jnp.arange(rows, dtype=jnp.int32)[:, None]
        * jnp.arange(cols, dtype=jnp.int32)[None, :]
        % length
    )
    angle = product.astype(jnp.float32) * (2.0 * math.pi / length)
    return (jnp.cos(angle), sign * jnp.sin(angle))


def mix_einsum(form, left, right):
    return jnp.einsum(form, left, right, precision=lax.Precision.HIGHEST)


def forward_spectrum(signal):
    chans, length = signal.shape
    total_len = 2 * length
    bits = total_len.bit_length() - 1
    outer_len = 2 ** (bits // 2)
    inner_len = total_len // outer_len
    half_outer = outer_len // 2
    folded = signal.reshape(chans, half_outer, inner_len)
    first_re, first_im = wave_table(outer_len, half_outer, outer_len, -1.0)
    mid_re = mix_einsum("kn,cna->cka", first_re, folded)
    mid_im = mix_einsum("kn,cna->cka", first_im, folded)
    twist_re, twist_im = wave_table(outer_len, inner_len, total_len, -1.0)
    rot_re = mid_re * twist_re - mid_im * twist_im
    rot_im = mid_re * twist_im + mid_im * twist_re
    last_re, last_im = wave_table(inner_len, inner_len, inner_len, -1.0)
    out_re = mix_einsum("cka,aj->ckj", rot_re, last_re) - mix_einsum("cka,aj->ckj", rot_im, last_im)
    out_im = mix_einsum("cka,aj->ckj", rot_re, last_im) + mix_einsum("cka,aj->ckj", rot_im, last_re)
    return (out_re, out_im)


def inverse_signal(spec_re, spec_im):
    chans, outer_len, inner_len = spec_re.shape
    total_len = outer_len * inner_len
    last_re, last_im = wave_table(inner_len, inner_len, inner_len, 1.0)
    mid_re = mix_einsum("ckj,ja->cka", spec_re, last_re) - mix_einsum(
        "ckj,ja->cka", spec_im, last_im
    )
    mid_im = mix_einsum("ckj,ja->cka", spec_re, last_im) + mix_einsum(
        "ckj,ja->cka", spec_im, last_re
    )
    twist_re, twist_im = wave_table(outer_len, inner_len, total_len, 1.0)
    rot_re = mid_re * twist_re - mid_im * twist_im
    rot_im = mid_re * twist_im + mid_im * twist_re
    first_re, first_im = wave_table(outer_len // 2, outer_len, outer_len, 1.0)
    signal = mix_einsum("nk,cka->cna", first_re, rot_re) - mix_einsum(
        "nk,cka->cna", first_im, rot_im
    )
    return signal.reshape(chans, -1) / total_len


def two_level_on_device(out_grad, gate_in, conv_in, filter_raw, out_weight):
    grad_rows = out_grad[0]
    gate_local = gate_in[0]
    conv_local = conv_in[0]
    unit_grad = lax.dot_general(
        out_weight,
        lax.all_gather(grad_rows, "tp", axis=0, tiled=True),
        (((1,), (1,)), ((), ())),
        preferred_element_type=jnp.float32,
    )
    gate_grad = (unit_grad * gate_local.astype(jnp.float32)).astype(jnp.bfloat16)
    gate_chan, conv_chan = (
        lax.all_to_all(gate_grad, "ctx", split_axis=0, concat_axis=1, tiled=True),
        lax.all_to_all(conv_local, "ctx", split_axis=0, concat_axis=1, tiled=True),
    )
    length = filter_raw.shape[1]
    norm_scale = 1.0 / math.sqrt(length)
    filt_re, filt_im = forward_spectrum(filter_raw * norm_scale)
    conv_re, conv_im = forward_spectrum(conv_chan.astype(jnp.float32))
    gate_re, gate_im = forward_spectrum(gate_chan.astype(jnp.float32))
    conv_out = inverse_signal(
        filt_re * conv_re - filt_im * conv_im, filt_re * conv_im + filt_im * conv_re
    ).astype(jnp.bfloat16)
    conv_grad = inverse_signal(
        filt_re * gate_re + filt_im * gate_im, filt_re * gate_im - filt_im * gate_re
    ).astype(jnp.bfloat16)
    cross_re = gate_re * conv_re + gate_im * conv_im
    cross_im = gate_im * conv_re - gate_re * conv_im
    back_out, back_grad = (
        lax.all_to_all(conv_out, "ctx", split_axis=1, concat_axis=0, tiled=True),
        lax.all_to_all(conv_grad, "ctx", split_axis=1, concat_axis=0, tiled=True),
    )
    gate_out = (unit_grad * back_out.astype(jnp.float32)).astype(jnp.bfloat16)
    summed_re, summed_im = (
        lax.psum_scatter(cross_re * norm_scale, "dp", scatter_dimension=0, tiled=True),
        lax.psum_scatter(cross_im * norm_scale, "dp", scatter_dimension=0, tiled=True),
    )
    filter_grad = inverse_signal(summed_re, summed_im)
    return (gate_out[None], back_grad[None], filter_grad)


TABLE_LIMIT_BYTES = 4 * 2**20
VMEM_BYTES = 24 * 2**20


def split_high_low(values):
    high = values.astype(ml_dtypes.bfloat16)
    low = (values - high.astype(np.float64)).astype(ml_dtypes.bfloat16)
    return high, low


@functools.lru_cache(maxsize=None)
def dense_tables(length):
    total = 2 * length
    time = np.arange(length)[:, None]
    freq = np.arange(length)[None, :]
    angle = (time * freq % total) * (2.0 * np.pi / total)
    even_odd = 1.0 - 2.0 * (np.arange(length) % 2)
    real, imag = np.cos(angle), -np.sin(angle)
    imag[:, 0] = even_odd
    weight = np.full((length, 1), 2.0 / total)
    weight[0] = 1.0 / total
    forward = np.concatenate([real, imag], axis=1)
    inverse = np.concatenate([real.T * weight, imag.T * weight], axis=0)
    return split_high_low(forward) + split_high_low(inverse)


def mm(left, right):
    return jnp.dot(left, right, preferred_element_type=jnp.float32)


def mm_nt(left, right):
    return lax.dot_general(left, right, (((1,), (1,)), ((), ())), preferred_element_type=jnp.float32)


def halves(values):
    high = values.astype(jnp.bfloat16)
    return high, (values - high.astype(jnp.float32)).astype(jnp.bfloat16)


def spectrum_product(left, right, conj_left):
    length = left.shape[1] // 2
    lr, li = left[:, :length], left[:, length:]
    rr, ri = right[:, :length], right[:, length:]
    ends = lax.broadcasted_iota(jnp.int32, lr.shape, 1) == 0
    both = li * ri
    if conj_left:
        real = lr * rr + jnp.where(ends, 0.0, both)
        imag = jnp.where(ends, both, lr * ri - li * rr)
    else:
        real = lr * rr - jnp.where(ends, 0.0, both)
        imag = jnp.where(ends, both, lr * ri + li * rr)
    return jnp.concatenate([real, imag], axis=1)


def inverse_dense(spec, inv_hi, inv_lo):
    high, low = halves(spec)
    return mm(high, inv_hi[...]) + mm(low, inv_hi[...]) + mm(high, inv_lo[...])


def place(index, size):
    return pl.ds(pl.multiple_of(index * size, size), size)


def offsets(parts):
    return [0, *reversed(range(1, parts))]


def gather_tokens(pieces, whole, here):
    step = pieces[0].shape[1]
    for k, piece in zip(offsets(len(pieces)), pieces):
        whole[:, place(here ^ k, step)] = piece[...]


def scatter_tokens(whole, pieces, here, order):
    step = pieces[0].shape[1]
    for k, piece in zip(order, pieces):
        piece[...] = whole[:, place(here ^ k, step)]


def blocks_kernel(source, *refs):
    out, sems = refs[:-1], refs[-1]
    here = lax.axis_index("ctx")
    rows = out[0].shape[0]
    copies = [
        pltpu.make_async_copy(source.at[place(here ^ k, rows), :], ref, sems.at[k])
        for k, ref in zip(offsets(len(out)), out)
    ]
    for copy in copies:
        copy.start()
    for copy in copies:
        copy.wait()


def filt_kernel(scale, filt, fwd_hi, fwd_lo, after_1, after_2, spec_filt):
    high, low = halves(filt[...] * scale)
    spec_filt[...] = mm(high, fwd_hi[...]) + mm(low, fwd_hi[...]) + mm(high, fwd_lo[...])


def spectrum_of(signal, fwd_hi, fwd_lo):
    return mm(signal, fwd_hi[...]) + mm(signal, fwd_lo[...])


def pair_rows(rows, mine):
    at = lax.axis_index("dp")
    return place(at if mine else 1 - at, rows)


def conv_kernel(parts, *refs):
    conv = refs[:parts]
    spec_filt, fwd_hi, fwd_lo, inv_hi, inv_lo = refs[parts : parts + 5]
    out = refs[parts + 5 : 2 * parts + 5]
    spec_conv, whole = refs[2 * parts + 5 :]
    here = lax.axis_index("ctx")
    gather_tokens(conv, whole, here)
    spec_conv[...] = spectrum_of(whole[...], fwd_hi, fwd_lo)
    product = spectrum_product(spec_filt[...], spec_conv[...], False)
    whole[...] = inverse_dense(product, inv_hi, inv_lo).astype(jnp.bfloat16)
    scatter_tokens(whole, out, here, offsets(parts))


def unit_kernel(parts, pieces, after, weight, gate, *refs):
    grads = refs[:pieces]
    unit = refs[pieces]
    out = refs[pieces + 1 : pieces + 1 + parts]
    rows_all = refs[pieces + 1 + parts]
    here, block = lax.axis_index("ctx"), lax.axis_index("tp")
    rows = grads[0].shape[0]
    half = rows_all.shape[1] // 2
    for k, ref in enumerate(grads[:3]):
        rows_all[place(block ^ k, rows), :] = ref[...]
    rows_all[place(block ^ 3, rows), :half] = grads[3][...]
    rows_all[place(block ^ 3, rows), half:] = grads[4][...]
    rows = out[0].shape[0]
    unit[...] = mm_nt(weight[...], rows_all[...])
    for k, ref in zip(offsets(parts), out):
        at = place(here ^ k, rows)
        ref[...] = (unit[at, :] * gate[at, :].astype(jnp.float32)).astype(jnp.bfloat16)


def grad_kernel(parts, *refs):
    gate = refs[:parts]
    spec_filt, fwd_hi, fwd_lo, inv_hi, inv_lo = refs[parts : parts + 5]
    out = refs[parts + 5 : 2 * parts + 5]
    spec_gate, whole = refs[2 * parts + 5 :]
    here = lax.axis_index("ctx")
    gather_tokens(gate, whole, here)
    spec_gate[...] = spectrum_of(whole[...], fwd_hi, fwd_lo)
    product = spectrum_product(spec_filt[...], spec_gate[...], True)
    whole[...] = inverse_dense(product, inv_hi, inv_lo).astype(jnp.bfloat16)
    scatter_tokens(whole, out, here, offsets(parts))


def filter_kernel(parts, scale, spec_conv, spec_gate, inv_hi, inv_lo, unit, *refs):
    back = refs[:parts]
    keep, *send, out, whole = refs[parts:]
    here = lax.axis_index("ctx")
    rows = back[0].shape[0]
    for k, ref in zip(offsets(parts), back):
        at = place(here ^ k, rows)
        out[at, :] = (unit[at, :] * ref[...].astype(jnp.float32)).astype(jnp.bfloat16)
    product = spectrum_product(spec_conv[...], spec_gate[...], True)
    whole[...] = inverse_dense(product, inv_hi, inv_lo) * scale
    rows = keep.shape[0]
    keep[...] = whole[pair_rows(rows, True), :]
    for i, ref in enumerate(send):
        step = ref.shape[0]
        at = pl.multiple_of(pair_rows(rows, False).start + i * step, step)
        ref[...] = whole[pl.ds(at, step), :].astype(jnp.bfloat16)


def last_kernel(parts, *refs):
    back, (low, high, keep, total, out) = refs[:parts], refs[parts:]
    step = low.shape[0]
    for i, ref in enumerate((low, high)):
        at = slice(i * step, (i + 1) * step)
        total[at, :] = keep[at, :] + ref[...].astype(jnp.float32)
    here = lax.axis_index("ctx")
    rows = back[0].shape[0]
    for k, ref in zip(offsets(parts), back):
        out[place(here ^ k, rows), :] = ref[...]


def call(kernel, outs, args, scratch=(), far=(), cost=1.0):
    vmem = pl.BlockSpec(memory_space=pltpu.VMEM)
    hbm = pl.BlockSpec(memory_space=pltpu.HBM)
    held = [
        pltpu.with_memory_space_constraint(a, pltpu.HBM) if i in far else a
        for i, a in enumerate(args)
    ]
    return pl.pallas_call(
        kernel,
        out_shape=outs,
        in_specs=[hbm if i in far else vmem for i in range(len(args))],
        out_specs=jax.tree.map(lambda _: vmem, outs),
        scratch_shapes=list(scratch),
        cost_estimate=pl.CostEstimate(
            flops=int(cost * 1e9), bytes_accessed=int(cost * 1e6), transcendentals=0
        ),
        compiler_params=pltpu.CompilerParams(vmem_limit_bytes=VMEM_BYTES),
    )(*held)


def dense_on_device(parts, groups, out_grad, gate_in, conv_in, filter_raw, out_weight):
    f32, bf16 = jnp.float32, jnp.bfloat16
    grad_rows, gate_local, conv_local = out_grad[0], gate_in[0], conv_in[0]
    chans, length = filter_raw.shape
    channels, tokens = conv_local.shape
    width = grad_rows.shape[1]
    scale = 1.0 / math.sqrt(length)
    tables = [jnp.asarray(t) for t in dense_tables(length)]
    shape = jax.ShapeDtypeStruct
    def swap(value, axis, size, k):
        return lax.ppermute(value, axis, [(i, i ^ k) for i in range(size)])

    def exchange(pieces, order):
        return [swap(p, "ctx", parts, k) if k else p for k, p in zip(order, pieces)]

    grad_1 = swap(grad_rows, "tp", groups, 1)
    grad_2 = swap(grad_rows, "tp", groups, 2)
    blocks = call(
        blocks_kernel,
        [shape((chans, tokens), bf16)] * parts,
        [conv_local],
        [pltpu.SemaphoreType.DMA((parts,))],
        far=(0,),
        cost=10.0,
    )
    conv_pieces = exchange(blocks, offsets(parts))
    grad_3a = swap(grad_1[:, : width // 2], "tp", groups, 2)
    grad_3b = swap(grad_2[:, width // 2 :], "tp", groups, 1)

    piece = shape((chans, tokens), bf16)
    spectrum = shape((chans, 2 * length), f32)
    whole = pltpu.VMEM((chans, length), bf16)
    spec_filt = call(
        functools.partial(filt_kernel, scale),
        spectrum,
        [filter_raw, *tables[:2], grad_1, grad_2],
        cost=2.0,
    )
    *conv_out, spec_conv = call(
        functools.partial(conv_kernel, parts),
        [piece] * parts + [spectrum],
        [*conv_pieces, spec_filt, *tables],
        [whole],
        cost=2.0,
    )
    conv_back = exchange(conv_out, offsets(parts))

    unit, *gate_pieces = call(
        functools.partial(unit_kernel, parts, 5),
        [shape((channels, tokens), f32)] + [piece] * parts,
        [conv_out[0], out_weight, gate_local, grad_rows, grad_1, grad_2, grad_3a, grad_3b],
        [pltpu.VMEM((groups * grad_rows.shape[0], width), bf16)],
    )
    gate_chan = exchange(gate_pieces, offsets(parts))
    *conv_grad, spec_gate = call(
        functools.partial(grad_kernel, parts),
        [piece] * parts + [spectrum],
        [*gate_chan, spec_filt, *tables],
        [whole],
    )
    grad_back = exchange(conv_grad, offsets(parts))
    half, local = shape((chans // 2, length), f32), shape((channels, tokens), bf16)
    quarter = shape((chans // 4, length), bf16)
    keep, send_low, send_high, gate_out = call(
        functools.partial(filter_kernel, parts, scale),
        [half, quarter, quarter, local],
        [spec_conv, spec_gate, *tables[2:], unit, *conv_back],
        [pltpu.VMEM((chans, length), f32)],
        cost=2.0,
    )
    filter_grad, conv_grad_out = call(
        functools.partial(last_kernel, parts),
        [half, local],
        [*grad_back, swap(send_low, "dp", 2, 1), swap(send_high, "dp", 2, 1), keep],
    )
    return (gate_out[None], conv_grad_out[None], filter_grad)


def solution(mesh):
    placed = (
        P("dp", ("ctx", "tp"), None),
        P("dp", "tp", "ctx"),
        P("dp", "tp", "ctx"),
        P(("tp", "ctx"), None),
        P("tp", None),
    )
    parts, groups, pair = mesh.shape["ctx"], mesh.shape["tp"], mesh.shape["dp"]

    def on_device(out_grad, gate_in, conv_in, filter_raw, out_weight):
        args = (out_grad, gate_in, conv_in, filter_raw, out_weight)
        table = 4 * filter_raw.shape[1] ** 2 * jnp.dtype(jnp.bfloat16).itemsize
        one_sequence = out_grad.shape[0] == 1
        power = parts & (parts - 1) == 0
        if one_sequence and power and parts > 1 and groups == 4 and pair == 2 and table <= TABLE_LIMIT_BYTES:
            return dense_on_device(parts, groups, *args)
        return two_level_on_device(*args)

    return jax.shard_map(
        on_device,
        mesh=mesh,
        in_specs=placed,
        out_specs=(P("dp", "tp", "ctx"), P("dp", "tp", "ctx"), P(("tp", "ctx", "dp"), None)),
        check_vma=False,
    )
```

```python
import functools
import math

import jax
import jax.numpy as jnp
import ml_dtypes
import numpy as np
from jax import lax
from jax.experimental import pallas as pl
from jax.experimental.pallas import tpu as pltpu
from jax.sharding import PartitionSpec as P


def wave_table(rows, cols, length, sign):
    product = (
        jnp.arange(rows, dtype=jnp.int32)[:, None]
        * jnp.arange(cols, dtype=jnp.int32)[None, :]
        % length
    )
    angle = product.astype(jnp.float32) * (2.0 * math.pi / length)
    return (jnp.cos(angle), sign * jnp.sin(angle))


def mix_einsum(form, left, right):
    return jnp.einsum(form, left, right, precision=lax.Precision.HIGHEST)


def forward_spectrum(signal):
    chans, length = signal.shape
    total_len = 2 * length
    bits = total_len.bit_length() - 1
    outer_len = 2 ** (bits // 2)
    inner_len = total_len // outer_len
    half_outer = outer_len // 2
    folded = signal.reshape(chans, half_outer, inner_len)
    first_re, first_im = wave_table(outer_len, half_outer, outer_len, -1.0)
    mid_re = mix_einsum("kn,cna->cka", first_re, folded)
    mid_im = mix_einsum("kn,cna->cka", first_im, folded)
    twist_re, twist_im = wave_table(outer_len, inner_len, total_len, -1.0)
    rot_re = mid_re * twist_re - mid_im * twist_im
    rot_im = mid_re * twist_im + mid_im * twist_re
    last_re, last_im = wave_table(inner_len, inner_len, inner_len, -1.0)
    out_re = mix_einsum("cka,aj->ckj", rot_re, last_re) - mix_einsum("cka,aj->ckj", rot_im, last_im)
    out_im = mix_einsum("cka,aj->ckj", rot_re, last_im) + mix_einsum("cka,aj->ckj", rot_im, last_re)
    return (out_re, out_im)


def inverse_signal(spec_re, spec_im):
    chans, outer_len, inner_len = spec_re.shape
    total_len = outer_len * inner_len
    last_re, last_im = wave_table(inner_len, inner_len, inner_len, 1.0)
    mid_re = mix_einsum("ckj,ja->cka", spec_re, last_re) - mix_einsum(
        "ckj,ja->cka", spec_im, last_im
    )
    mid_im = mix_einsum("ckj,ja->cka", spec_re, last_im) + mix_einsum(
        "ckj,ja->cka", spec_im, last_re
    )
    twist_re, twist_im = wave_table(outer_len, inner_len, total_len, 1.0)
    rot_re = mid_re * twist_re - mid_im * twist_im
    rot_im = mid_re * twist_im + mid_im * twist_re
    first_re, first_im = wave_table(outer_len // 2, outer_len, outer_len, 1.0)
    signal = mix_einsum("nk,cka->cna", first_re, rot_re) - mix_einsum(
        "nk,cka->cna", first_im, rot_im
    )
    return signal.reshape(chans, -1) / total_len


def two_level_on_device(out_grad, gate_in, conv_in, filter_raw, out_weight):
    grad_rows = out_grad[0]
    gate_local = gate_in[0]
    conv_local = conv_in[0]
    unit_grad = lax.dot_general(
        out_weight,
        lax.all_gather(grad_rows, "tp", axis=0, tiled=True),
        (((1,), (1,)), ((), ())),
        preferred_element_type=jnp.float32,
    )
    gate_grad = (unit_grad * gate_local.astype(jnp.float32)).astype(jnp.bfloat16)
    gate_chan, conv_chan = (
        lax.all_to_all(gate_grad, "ctx", split_axis=0, concat_axis=1, tiled=True),
        lax.all_to_all(conv_local, "ctx", split_axis=0, concat_axis=1, tiled=True),
    )
    length = filter_raw.shape[1]
    norm_scale = 1.0 / math.sqrt(length)
    filt_re, filt_im = forward_spectrum(filter_raw * norm_scale)
    conv_re, conv_im = forward_spectrum(conv_chan.astype(jnp.float32))
    gate_re, gate_im = forward_spectrum(gate_chan.astype(jnp.float32))
    conv_out = inverse_signal(
        filt_re * conv_re - filt_im * conv_im, filt_re * conv_im + filt_im * conv_re
    ).astype(jnp.bfloat16)
    conv_grad = inverse_signal(
        filt_re * gate_re + filt_im * gate_im, filt_re * gate_im - filt_im * gate_re
    ).astype(jnp.bfloat16)
    cross_re = gate_re * conv_re + gate_im * conv_im
    cross_im = gate_im * conv_re - gate_re * conv_im
    back_out, back_grad = (
        lax.all_to_all(conv_out, "ctx", split_axis=1, concat_axis=0, tiled=True),
        lax.all_to_all(conv_grad, "ctx", split_axis=1, concat_axis=0, tiled=True),
    )
    gate_out = (unit_grad * back_out.astype(jnp.float32)).astype(jnp.bfloat16)
    summed_re, summed_im = (
        lax.psum_scatter(cross_re * norm_scale, "dp", scatter_dimension=0, tiled=True),
        lax.psum_scatter(cross_im * norm_scale, "dp", scatter_dimension=0, tiled=True),
    )
    filter_grad = inverse_signal(summed_re, summed_im)
    return (gate_out[None], back_grad[None], filter_grad)


TABLE_LIMIT_BYTES = 4 * 2**20
VMEM_BYTES = 24 * 2**20


def split_high_low(values):
    high = values.astype(ml_dtypes.bfloat16)
    low = (values - high.astype(np.float64)).astype(ml_dtypes.bfloat16)
    return high, low


@functools.lru_cache(maxsize=None)
def dense_tables(length):
    total = 2 * length
    time = np.arange(length)[:, None]
    freq = np.arange(length)[None, :]
    angle = (time * freq % total) * (2.0 * np.pi / total)
    even_odd = 1.0 - 2.0 * (np.arange(length) % 2)
    real, imag = np.cos(angle), -np.sin(angle)
    imag[:, 0] = even_odd
    weight = np.full((length, 1), 2.0 / total)
    weight[0] = 1.0 / total
    forward = np.concatenate([real, imag], axis=1)
    inverse = np.concatenate([real.T * weight, imag.T * weight], axis=0)
    return split_high_low(forward) + split_high_low(inverse)


def mm(left, right):
    return jnp.dot(left, right, preferred_element_type=jnp.float32)


def mm_nt(left, right):
    return lax.dot_general(left, right, (((1,), (1,)), ((), ())), preferred_element_type=jnp.float32)


def halves(values):
    high = values.astype(jnp.bfloat16)
    return high, (values - high.astype(jnp.float32)).astype(jnp.bfloat16)


def spectrum_product(left, right, conj_left):
    length = left.shape[1] // 2
    lr, li = left[:, :length], left[:, length:]
    rr, ri = right[:, :length], right[:, length:]
    ends = lax.broadcasted_iota(jnp.int32, lr.shape, 1) == 0
    both = li * ri
    if conj_left:
        real = lr * rr + jnp.where(ends, 0.0, both)
        imag = jnp.where(ends, both, lr * ri - li * rr)
    else:
        real = lr * rr - jnp.where(ends, 0.0, both)
        imag = jnp.where(ends, both, lr * ri + li * rr)
    return jnp.concatenate([real, imag], axis=1)


def inverse_dense(spec, inv_hi, inv_lo):
    high, low = halves(spec)
    return mm(high, inv_hi[...]) + mm(low, inv_hi[...]) + mm(high, inv_lo[...])


def place(index, size):
    return pl.ds(pl.multiple_of(index * size, size), size)


def offsets(parts):
    return [0, *reversed(range(1, parts))]


def back_offsets(parts):
    return [0, parts - 1, *range(1, parts - 1)]


def gather_tokens(pieces, whole, here):
    step = pieces[0].shape[1]
    for k, piece in zip(offsets(len(pieces)), pieces):
        whole[:, place(here ^ k, step)] = piece[...]


def scatter_tokens(whole, pieces, here, order):
    step = pieces[0].shape[1]
    for k, piece in zip(order, pieces):
        piece[...] = whole[:, place(here ^ k, step)]


def blocks_kernel(source, *refs):
    out, sems = refs[:-1], refs[-1]
    here = lax.axis_index("ctx")
    rows = out[0].shape[0]
    copies = [
        pltpu.make_async_copy(source.at[place(here ^ k, rows), :], ref, sems.at[k])
        for k, ref in zip(offsets(len(out)), out)
    ]
    for copy in copies:
        copy.start()
    for copy in copies:
        copy.wait()


def filt_kernel(scale, filt, fwd_hi, fwd_lo, after_1, after_2, spec_filt):
    high, low = halves(filt[...] * scale)
    spec_filt[...] = mm(high, fwd_hi[...]) + mm(low, fwd_hi[...]) + mm(high, fwd_lo[...])


def spectrum_of(signal, fwd_hi, fwd_lo):
    return mm(signal, fwd_hi[...]) + mm(signal, fwd_lo[...])


def pair_rows(rows, mine):
    at = lax.axis_index("dp")
    return place(at if mine else 1 - at, rows)


def conv_kernel(parts, *refs):
    conv = refs[:parts]
    spec_filt, fwd_hi, fwd_lo, inv_hi, inv_lo = refs[parts : parts + 5]
    out = refs[parts + 5 : 2 * parts + 5]
    spec_conv, whole = refs[2 * parts + 5 :]
    here = lax.axis_index("ctx")
    gather_tokens(conv, whole, here)
    spec_conv[...] = spectrum_of(whole[...], fwd_hi, fwd_lo)
    product = spectrum_product(spec_filt[...], spec_conv[...], False)
    whole[...] = inverse_dense(product, inv_hi, inv_lo).astype(jnp.bfloat16)
    scatter_tokens(whole, out, here, back_offsets(parts))


def unit_kernel(parts, pieces, after, weight, gate, *refs):
    grads = refs[:pieces]
    unit = refs[pieces]
    out = refs[pieces + 1 : pieces + 1 + parts]
    rows_all = refs[pieces + 1 + parts]
    here, block = lax.axis_index("ctx"), lax.axis_index("tp")
    rows = grads[0].shape[0]
    cut = grads[3].shape[1]
    for k, ref in enumerate(grads[:3]):
        rows_all[place(block ^ k, rows), :] = ref[...]
    rows_all[place(block ^ 3, rows), :cut] = grads[3][...]
    rows_all[place(block ^ 3, rows), cut:] = grads[4][...]
    rows = out[0].shape[0]
    for k, ref in zip(offsets(parts), out):
        at = place(here ^ k, rows)
        got = mm_nt(weight[at, :], rows_all[...])
        unit[at, :] = got
        ref[...] = (got * gate[at, :].astype(jnp.float32)).astype(jnp.bfloat16)


def grad_kernel(parts, *refs):
    gate = refs[:parts]
    spec_filt, fwd_hi, fwd_lo, inv_hi, inv_lo = refs[parts : parts + 5]
    out = refs[parts + 5 : 2 * parts + 5]
    spec_gate, whole = refs[2 * parts + 5 :]
    here = lax.axis_index("ctx")
    gather_tokens(gate, whole, here)
    spec_gate[...] = spectrum_of(whole[...], fwd_hi, fwd_lo)
    product = spectrum_product(spec_filt[...], spec_gate[...], True)
    whole[...] = inverse_dense(product, inv_hi, inv_lo).astype(jnp.bfloat16)
    scatter_tokens(whole, out, here, offsets(parts))


def filter_kernel(parts, scale, spec_conv, spec_gate, inv_hi, inv_lo, unit, *refs):
    back = refs[:parts]
    keep, *send, out, whole = refs[parts:]
    here = lax.axis_index("ctx")
    rows = back[0].shape[0]
    for k, ref in zip(back_offsets(parts), back):
        at = place(here ^ k, rows)
        out[at, :] = (unit[at, :] * ref[...].astype(jnp.float32)).astype(jnp.bfloat16)
    product = spectrum_product(spec_conv[...], spec_gate[...], True)
    whole[...] = inverse_dense(product, inv_hi, inv_lo) * scale
    rows = keep.shape[0]
    keep[...] = whole[pair_rows(rows, True), :]
    for i, ref in enumerate(send):
        step = ref.shape[0]
        at = pl.multiple_of(pair_rows(rows, False).start + i * step, step)
        ref[...] = whole[pl.ds(at, step), :].astype(jnp.bfloat16)


def last_kernel(parts, *refs):
    back, (low, high, keep, total, out) = refs[:parts], refs[parts:]
    step = low.shape[0]
    for i, ref in enumerate((low, high)):
        at = slice(i * step, (i + 1) * step)
        total[at, :] = keep[at, :] + ref[...].astype(jnp.float32)
    here = lax.axis_index("ctx")
    rows = back[0].shape[0]
    for k, ref in zip(offsets(parts), back):
        out[place(here ^ k, rows), :] = ref[...]


def call(kernel, outs, args, scratch=(), far=(), cost=1.0):
    vmem = pl.BlockSpec(memory_space=pltpu.VMEM)
    hbm = pl.BlockSpec(memory_space=pltpu.HBM)
    held = [
        pltpu.with_memory_space_constraint(a, pltpu.HBM) if i in far else a
        for i, a in enumerate(args)
    ]
    return pl.pallas_call(
        kernel,
        out_shape=outs,
        in_specs=[hbm if i in far else vmem for i in range(len(args))],
        out_specs=jax.tree.map(lambda _: vmem, outs),
        scratch_shapes=list(scratch),
        cost_estimate=pl.CostEstimate(
            flops=int(cost * 1e9), bytes_accessed=int(cost * 1e6), transcendentals=0
        ),
        compiler_params=pltpu.CompilerParams(vmem_limit_bytes=VMEM_BYTES),
    )(*held)


def dense_on_device(parts, groups, out_grad, gate_in, conv_in, filter_raw, out_weight):
    f32, bf16 = jnp.float32, jnp.bfloat16
    grad_rows, gate_local, conv_local = out_grad[0], gate_in[0], conv_in[0]
    chans, length = filter_raw.shape
    channels, tokens = conv_local.shape
    width = grad_rows.shape[1]
    scale = 1.0 / math.sqrt(length)
    tables = [jnp.asarray(t) for t in dense_tables(length)]
    shape = jax.ShapeDtypeStruct
    def swap(value, axis, size, k):
        return lax.ppermute(value, axis, [(i, i ^ k) for i in range(size)])

    def exchange(pieces, order):
        return [swap(p, "ctx", parts, k) if k else p for k, p in zip(order, pieces)]

    grad_1 = swap(grad_rows, "tp", groups, 1)
    grad_2 = swap(grad_rows, "tp", groups, 2)
    blocks = call(
        blocks_kernel,
        [shape((chans, tokens), bf16)] * parts,
        [conv_local],
        [pltpu.SemaphoreType.DMA((parts,))],
        far=(0,),
        cost=10.0,
    )
    conv_pieces = exchange(blocks, offsets(parts))
    cut = width * 3 // 8
    grad_3a = swap(grad_1[:, :cut], "tp", groups, 2)
    grad_3b = swap(grad_2[:, cut:], "tp", groups, 1)

    piece = shape((chans, tokens), bf16)
    spectrum = shape((chans, 2 * length), f32)
    whole = pltpu.VMEM((chans, length), bf16)
    spec_filt = call(
        functools.partial(filt_kernel, scale),
        spectrum,
        [filter_raw, *tables[:2], grad_1, grad_2],
        cost=2.0,
    )
    *conv_out, spec_conv = call(
        functools.partial(conv_kernel, parts),
        [piece] * parts + [spectrum],
        [*conv_pieces, spec_filt, *tables],
        [whole],
        cost=2.0,
    )
    conv_back = exchange(conv_out, back_offsets(parts))

    unit, *gate_pieces = call(
        functools.partial(unit_kernel, parts, 5),
        [shape((channels, tokens), f32)] + [piece] * parts,
        [conv_out[0], out_weight, gate_local, grad_rows, grad_1, grad_2, grad_3a, grad_3b],
        [pltpu.VMEM((groups * grad_rows.shape[0], width), bf16)],
    )
    gate_chan = exchange(gate_pieces, offsets(parts))
    *conv_grad, spec_gate = call(
        functools.partial(grad_kernel, parts),
        [piece] * parts + [spectrum],
        [*gate_chan, spec_filt, *tables],
        [whole],
    )
    grad_back = exchange(conv_grad, offsets(parts))
    half, local = shape((chans // 2, length), f32), shape((channels, tokens), bf16)
    quarter = shape((chans // 4, length), bf16)
    keep, send_low, send_high, gate_out = call(
        functools.partial(filter_kernel, parts, scale),
        [half, quarter, quarter, local],
        [spec_conv, spec_gate, *tables[2:], unit, *conv_back],
        [pltpu.VMEM((chans, length), f32)],
        cost=2.0,
    )
    filter_grad, conv_grad_out = call(
        functools.partial(last_kernel, parts),
        [half, local],
        [*grad_back, swap(send_low, "dp", 2, 1), swap(send_high, "dp", 2, 1), keep],
    )
    return (gate_out[None], conv_grad_out[None], filter_grad)


def solution(mesh):
    placed = (
        P("dp", ("ctx", "tp"), None),
        P("dp", "tp", "ctx"),
        P("dp", "tp", "ctx"),
        P(("tp", "ctx"), None),
        P("tp", None),
    )
    parts, groups, pair = mesh.shape["ctx"], mesh.shape["tp"], mesh.shape["dp"]

    def on_device(out_grad, gate_in, conv_in, filter_raw, out_weight):
        args = (out_grad, gate_in, conv_in, filter_raw, out_weight)
        table = 4 * filter_raw.shape[1] ** 2 * jnp.dtype(jnp.bfloat16).itemsize
        one_sequence = out_grad.shape[0] == 1
        power = parts & (parts - 1) == 0
        if one_sequence and power and parts > 1 and groups == 4 and pair == 2 and table <= TABLE_LIMIT_BYTES:
            return dense_on_device(parts, groups, *args)
        return two_level_on_device(*args)

    return jax.shard_map(
        on_device,
        mesh=mesh,
        in_specs=placed,
        out_specs=(P("dp", "tp", "ctx"), P("dp", "tp", "ctx"), P(("tp", "ctx", "dp"), None)),
        check_vma=False,
    )
```

```python
import functools
import math

import jax
import jax.numpy as jnp
import ml_dtypes
import numpy as np
from jax import lax
from jax.experimental import pallas as pl
from jax.experimental.pallas import tpu as pltpu
from jax.sharding import PartitionSpec as P


def wave_table(rows, cols, length, sign):
    product = (
        jnp.arange(rows, dtype=jnp.int32)[:, None]
        * jnp.arange(cols, dtype=jnp.int32)[None, :]
        % length
    )
    angle = product.astype(jnp.float32) * (2.0 * math.pi / length)
    return (jnp.cos(angle), sign * jnp.sin(angle))


def mix_einsum(form, left, right):
    return jnp.einsum(form, left, right, precision=lax.Precision.HIGHEST)


def forward_spectrum(signal):
    chans, length = signal.shape
    total_len = 2 * length
    bits = total_len.bit_length() - 1
    outer_len = 2 ** (bits // 2)
    inner_len = total_len // outer_len
    half_outer = outer_len // 2
    folded = signal.reshape(chans, half_outer, inner_len)
    first_re, first_im = wave_table(outer_len, half_outer, outer_len, -1.0)
    mid_re = mix_einsum("kn,cna->cka", first_re, folded)
    mid_im = mix_einsum("kn,cna->cka", first_im, folded)
    twist_re, twist_im = wave_table(outer_len, inner_len, total_len, -1.0)
    rot_re = mid_re * twist_re - mid_im * twist_im
    rot_im = mid_re * twist_im + mid_im * twist_re
    last_re, last_im = wave_table(inner_len, inner_len, inner_len, -1.0)
    out_re = mix_einsum("cka,aj->ckj", rot_re, last_re) - mix_einsum("cka,aj->ckj", rot_im, last_im)
    out_im = mix_einsum("cka,aj->ckj", rot_re, last_im) + mix_einsum("cka,aj->ckj", rot_im, last_re)
    return (out_re, out_im)


def inverse_signal(spec_re, spec_im):
    chans, outer_len, inner_len = spec_re.shape
    total_len = outer_len * inner_len
    last_re, last_im = wave_table(inner_len, inner_len, inner_len, 1.0)
    mid_re = mix_einsum("ckj,ja->cka", spec_re, last_re) - mix_einsum(
        "ckj,ja->cka", spec_im, last_im
    )
    mid_im = mix_einsum("ckj,ja->cka", spec_re, last_im) + mix_einsum(
        "ckj,ja->cka", spec_im, last_re
    )
    twist_re, twist_im = wave_table(outer_len, inner_len, total_len, 1.0)
    rot_re = mid_re * twist_re - mid_im * twist_im
    rot_im = mid_re * twist_im + mid_im * twist_re
    first_re, first_im = wave_table(outer_len // 2, outer_len, outer_len, 1.0)
    signal = mix_einsum("nk,cka->cna", first_re, rot_re) - mix_einsum(
        "nk,cka->cna", first_im, rot_im
    )
    return signal.reshape(chans, -1) / total_len


def two_level_on_device(out_grad, gate_in, conv_in, filter_raw, out_weight):
    grad_rows = out_grad[0]
    gate_local = gate_in[0]
    conv_local = conv_in[0]
    unit_grad = lax.dot_general(
        out_weight,
        lax.all_gather(grad_rows, "tp", axis=0, tiled=True),
        (((1,), (1,)), ((), ())),
        preferred_element_type=jnp.float32,
    )
    gate_grad = (unit_grad * gate_local.astype(jnp.float32)).astype(jnp.bfloat16)
    gate_chan, conv_chan = (
        lax.all_to_all(gate_grad, "ctx", split_axis=0, concat_axis=1, tiled=True),
        lax.all_to_all(conv_local, "ctx", split_axis=0, concat_axis=1, tiled=True),
    )
    length = filter_raw.shape[1]
    norm_scale = 1.0 / math.sqrt(length)
    filt_re, filt_im = forward_spectrum(filter_raw * norm_scale)
    conv_re, conv_im = forward_spectrum(conv_chan.astype(jnp.float32))
    gate_re, gate_im = forward_spectrum(gate_chan.astype(jnp.float32))
    conv_out = inverse_signal(
        filt_re * conv_re - filt_im * conv_im, filt_re * conv_im + filt_im * conv_re
    ).astype(jnp.bfloat16)
    conv_grad = inverse_signal(
        filt_re * gate_re + filt_im * gate_im, filt_re * gate_im - filt_im * gate_re
    ).astype(jnp.bfloat16)
    cross_re = gate_re * conv_re + gate_im * conv_im
    cross_im = gate_im * conv_re - gate_re * conv_im
    back_out, back_grad = (
        lax.all_to_all(conv_out, "ctx", split_axis=1, concat_axis=0, tiled=True),
        lax.all_to_all(conv_grad, "ctx", split_axis=1, concat_axis=0, tiled=True),
    )
    gate_out = (unit_grad * back_out.astype(jnp.float32)).astype(jnp.bfloat16)
    summed_re, summed_im = (
        lax.psum_scatter(cross_re * norm_scale, "dp", scatter_dimension=0, tiled=True),
        lax.psum_scatter(cross_im * norm_scale, "dp", scatter_dimension=0, tiled=True),
    )
    filter_grad = inverse_signal(summed_re, summed_im)
    return (gate_out[None], back_grad[None], filter_grad)


TABLE_LIMIT_BYTES = 4 * 2**20
VMEM_BYTES = 24 * 2**20


def split_high_low(values):
    high = values.astype(ml_dtypes.bfloat16)
    low = (values - high.astype(np.float64)).astype(ml_dtypes.bfloat16)
    return high, low


@functools.lru_cache(maxsize=None)
def dense_tables(length):
    total = 2 * length
    time = np.arange(length)[:, None]
    freq = np.arange(length)[None, :]
    angle = (time * freq % total) * (2.0 * np.pi / total)
    even_odd = 1.0 - 2.0 * (np.arange(length) % 2)
    real, imag = np.cos(angle), -np.sin(angle)
    imag[:, 0] = even_odd
    weight = np.full((length, 1), 2.0 / total)
    weight[0] = 1.0 / total
    forward = np.concatenate([real, imag], axis=1)
    inverse = np.concatenate([real.T * weight, imag.T * weight], axis=0)
    return split_high_low(forward) + split_high_low(inverse)


def mm(left, right):
    return jnp.dot(left, right, preferred_element_type=jnp.float32)


def mm_nt(left, right):
    return lax.dot_general(left, right, (((1,), (1,)), ((), ())), preferred_element_type=jnp.float32)


def halves(values):
    high = values.astype(jnp.bfloat16)
    return high, (values - high.astype(jnp.float32)).astype(jnp.bfloat16)


def spectrum_product(left, right, conj_left):
    length = left.shape[1] // 2
    lr, li = left[:, :length], left[:, length:]
    rr, ri = right[:, :length], right[:, length:]
    ends = lax.broadcasted_iota(jnp.int32, lr.shape, 1) == 0
    both = li * ri
    if conj_left:
        real = lr * rr + jnp.where(ends, 0.0, both)
        imag = jnp.where(ends, both, lr * ri - li * rr)
    else:
        real = lr * rr - jnp.where(ends, 0.0, both)
        imag = jnp.where(ends, both, lr * ri + li * rr)
    return jnp.concatenate([real, imag], axis=1)


def inverse_dense(spec, inv_hi, inv_lo):
    high, low = halves(spec)
    return mm(high, inv_hi[...]) + mm(low, inv_hi[...]) + mm(high, inv_lo[...])


def place(index, size):
    return pl.ds(pl.multiple_of(index * size, size), size)


def offsets(parts):
    return [0, *reversed(range(1, parts))]


def middle_offsets(parts):
    return [0, *range(parts // 2, parts), *range(1, parts // 2)]


def gather_tokens(pieces, whole, here):
    step = pieces[0].shape[1]
    for k, piece in zip(offsets(len(pieces)), pieces):
        whole[:, place(here ^ k, step)] = piece[...]


def scatter_tokens(whole, pieces, here, order):
    step = pieces[0].shape[1]
    for k, piece in zip(order, pieces):
        piece[...] = whole[:, place(here ^ k, step)]


def blocks_kernel(source, *refs):
    out, sems = refs[:-1], refs[-1]
    here = lax.axis_index("ctx")
    rows = out[0].shape[0]
    copies = [
        pltpu.make_async_copy(source.at[place(here ^ k, rows), :], ref, sems.at[k])
        for k, ref in zip(offsets(len(out)), out)
    ]
    for copy in copies:
        copy.start()
    for copy in copies:
        copy.wait()


def filt_kernel(scale, filt, fwd_hi, fwd_lo, after_1, after_2, spec_filt):
    high, low = halves(filt[...] * scale)
    spec_filt[...] = mm(high, fwd_hi[...]) + mm(low, fwd_hi[...]) + mm(high, fwd_lo[...])


def spectrum_of(signal, fwd_hi, fwd_lo):
    return mm(signal, fwd_hi[...]) + mm(signal, fwd_lo[...])


def pair_rows(rows, mine):
    at = lax.axis_index("dp")
    return place(at if mine else 1 - at, rows)


def conv_kernel(parts, *refs):
    conv = refs[:parts]
    spec_filt, fwd_hi, fwd_lo, inv_hi, inv_lo = refs[parts : parts + 5]
    out = refs[parts + 5 : 2 * parts + 5]
    spec_conv, whole = refs[2 * parts + 5 :]
    here = lax.axis_index("ctx")
    gather_tokens(conv, whole, here)
    spec_conv[...] = spectrum_of(whole[...], fwd_hi, fwd_lo)
    product = spectrum_product(spec_filt[...], spec_conv[...], False)
    whole[...] = inverse_dense(product, inv_hi, inv_lo).astype(jnp.bfloat16)
    scatter_tokens(whole, out, here, range(parts))


def unit_rows(order, weight, gate, rows_all, unit, out):
    here = lax.axis_index("ctx")
    for k, grad, ref in zip(order, unit, out):
        rows = grad.shape[0]
        at = place(here ^ k, rows)
        got = mm_nt(weight[at, :], rows_all[...])
        grad[...] = got
        ref[...] = (got * gate[at, :].astype(jnp.float32)).astype(jnp.bfloat16)


def far_unit_kernel(order, pieces, after, weight, gate, *refs):
    grads, count = refs[:pieces], len(order)
    unit, out, rows_all = refs[pieces : pieces + count], refs[pieces + count : -1], refs[-1]
    block = lax.axis_index("tp")
    rows = grads[0].shape[0]
    cut = grads[3].shape[1]
    for k, ref in enumerate(grads[:3]):
        rows_all[place(block ^ k, rows), :] = ref[...]
    rows_all[place(block ^ 3, rows), :cut] = grads[3][...]
    rows_all[place(block ^ 3, rows), cut:] = grads[4][...]
    unit_rows(order, weight, gate, rows_all, unit, out)


def own_unit_kernel(order, weight, gate, rows_all, unit, out):
    unit_rows(order, weight, gate, rows_all, [unit], [out])


def grad_kernel(parts, *refs):
    gate = refs[:parts]
    spec_filt, fwd_hi, fwd_lo, inv_hi, inv_lo = refs[parts : parts + 5]
    out = refs[parts + 5 : 2 * parts + 5]
    spec_gate, whole = refs[2 * parts + 5 :]
    here = lax.axis_index("ctx")
    gather_tokens(gate, whole, here)
    spec_gate[...] = spectrum_of(whole[...], fwd_hi, fwd_lo)
    product = spectrum_product(spec_filt[...], spec_gate[...], True)
    whole[...] = inverse_dense(product, inv_hi, inv_lo).astype(jnp.bfloat16)
    scatter_tokens(whole, out, here, middle_offsets(parts))


def filter_kernel(parts, scale, spec_conv, spec_gate, inv_hi, inv_lo, *refs):
    keep, *send, whole = refs[parts:]
    product = spectrum_product(spec_conv[...], spec_gate[...], True)
    whole[...] = inverse_dense(product, inv_hi, inv_lo) * scale
    rows = keep.shape[0]
    keep[...] = whole[pair_rows(rows, True), :]
    for i, ref in enumerate(send):
        step = ref.shape[0]
        at = pl.multiple_of(pair_rows(rows, False).start + i * step, step)
        ref[...] = whole[pl.ds(at, step), :].astype(jnp.bfloat16)


def gate_kernel(parts, *refs):
    unit, back, out = refs[:parts], refs[parts : 2 * parts], refs[2 * parts]
    here = lax.axis_index("ctx")
    rows = back[0].shape[0]
    for k, grad, ref in zip(range(parts), unit, back):
        gated = grad[...] * ref[...].astype(jnp.float32)
        out[place(here ^ k, rows), :] = gated.astype(jnp.bfloat16)


def last_kernel(parts, *refs):
    back, (low, high, keep, total, out) = refs[:parts], refs[parts:]
    step = low.shape[0]
    for i, ref in enumerate((low, high)):
        at = slice(i * step, (i + 1) * step)
        total[at, :] = keep[at, :] + ref[...].astype(jnp.float32)
    here = lax.axis_index("ctx")
    rows = back[0].shape[0]
    for k, ref in zip(middle_offsets(parts), back):
        out[place(here ^ k, rows), :] = ref[...]


def call(kernel, outs, args, scratch=(), far=(), cost=1.0):
    vmem = pl.BlockSpec(memory_space=pltpu.VMEM)
    hbm = pl.BlockSpec(memory_space=pltpu.HBM)
    held = [
        pltpu.with_memory_space_constraint(a, pltpu.HBM) if i in far else a
        for i, a in enumerate(args)
    ]
    return pl.pallas_call(
        kernel,
        out_shape=outs,
        in_specs=[hbm if i in far else vmem for i in range(len(args))],
        out_specs=jax.tree.map(lambda _: vmem, outs),
        scratch_shapes=list(scratch),
        cost_estimate=pl.CostEstimate(
            flops=int(cost * 1e9), bytes_accessed=int(cost * 1e6), transcendentals=0
        ),
        compiler_params=pltpu.CompilerParams(vmem_limit_bytes=VMEM_BYTES),
    )(*held)


def dense_on_device(parts, groups, out_grad, gate_in, conv_in, filter_raw, out_weight):
    f32, bf16 = jnp.float32, jnp.bfloat16
    grad_rows, gate_local, conv_local = out_grad[0], gate_in[0], conv_in[0]
    chans, length = filter_raw.shape
    channels, tokens = conv_local.shape
    width = grad_rows.shape[1]
    scale = 1.0 / math.sqrt(length)
    tables = [jnp.asarray(t) for t in dense_tables(length)]
    shape = jax.ShapeDtypeStruct

    def swap(value, axis, size, k):
        return lax.ppermute(value, axis, [(i, i ^ k) for i in range(size)])

    def exchange(pieces, order):
        return [swap(p, "ctx", parts, k) if k else p for k, p in zip(order, pieces)]

    grad_1 = swap(grad_rows, "tp", groups, 1)
    grad_2 = swap(grad_rows, "tp", groups, 2)
    blocks = call(
        blocks_kernel,
        [shape((chans, tokens), bf16)] * parts,
        [conv_local],
        [pltpu.SemaphoreType.DMA((parts,))],
        far=(0,),
        cost=10.0,
    )
    conv_pieces = exchange(blocks, offsets(parts))
    cut = width // 16 * 5
    grad_3a = swap(grad_1[:, :cut], "tp", groups, 2)
    grad_3b = swap(grad_2[:, cut:], "tp", groups, 1)

    piece = shape((chans, tokens), bf16)
    spectrum = shape((chans, 2 * length), f32)
    whole = pltpu.VMEM((chans, length), bf16)
    spec_filt = call(
        functools.partial(filt_kernel, scale),
        spectrum,
        [filter_raw, *tables[:2], grad_1, grad_2],
        cost=2.0,
    )
    *conv_out, spec_conv = call(
        functools.partial(conv_kernel, parts),
        [piece] * parts + [spectrum],
        [*conv_pieces, spec_filt, *tables],
        [whole],
        cost=2.0,
    )

    away = offsets(parts)[1:]
    grad_all = shape((groups * grad_rows.shape[0], width), bf16)
    unit_piece = shape((chans, tokens), f32)
    *far, grad_all = call(
        functools.partial(far_unit_kernel, away, 5),
        [unit_piece] * len(away) + [piece] * len(away) + [grad_all],
        [conv_out[0], out_weight, gate_local, grad_rows, grad_1, grad_2, grad_3a, grad_3b],
    )
    unit_own, gate_own = call(
        functools.partial(own_unit_kernel, [0]),
        [unit_piece, piece],
        [out_weight, gate_local, grad_all],
    )
    *conv_out, gate_own = lax.optimization_barrier((*conv_out, gate_own))
    conv_back = exchange(conv_out, range(parts))
    gate_chan = exchange([gate_own, *far[len(away) :]], offsets(parts))
    unit = dict(zip(offsets(parts), [unit_own, *far[: len(away)]]))
    *conv_grad, spec_gate = call(
        functools.partial(grad_kernel, parts),
        [piece] * parts + [spectrum],
        [*gate_chan, spec_filt, *tables],
        [whole],
    )
    grad_back = exchange(conv_grad, middle_offsets(parts))
    half, local = shape((chans // 2, length), f32), shape((channels, tokens), bf16)
    quarter = shape((chans // 4, length), bf16)
    gate_out = call(
        functools.partial(gate_kernel, parts),
        local,
        [*(unit[k] for k in range(parts)), *conv_back],
    )
    keep, send_low, send_high = call(
        functools.partial(filter_kernel, parts, scale),
        [half, quarter, quarter],
        [spec_conv, spec_gate, *tables[2:], *conv_back],
        [pltpu.VMEM((chans, length), f32)],
        cost=2.0,
    )
    filter_grad, conv_grad_out = call(
        functools.partial(last_kernel, parts),
        [half, local],
        [*grad_back, swap(send_low, "dp", 2, 1), swap(send_high, "dp", 2, 1), keep],
    )
    return (gate_out[None], conv_grad_out[None], filter_grad)


def solution(mesh):
    placed = (
        P("dp", ("ctx", "tp"), None),
        P("dp", "tp", "ctx"),
        P("dp", "tp", "ctx"),
        P(("tp", "ctx"), None),
        P("tp", None),
    )
    parts, groups, pair = mesh.shape["ctx"], mesh.shape["tp"], mesh.shape["dp"]

    def on_device(out_grad, gate_in, conv_in, filter_raw, out_weight):
        args = (out_grad, gate_in, conv_in, filter_raw, out_weight)
        table = 4 * filter_raw.shape[1] ** 2 * jnp.dtype(jnp.bfloat16).itemsize
        one_sequence = out_grad.shape[0] == 1
        power = parts & (parts - 1) == 0
        if one_sequence and power and parts > 1 and groups == 4 and pair == 2 and table <= TABLE_LIMIT_BYTES:
            return dense_on_device(parts, groups, *args)
        return two_level_on_device(*args)

    return jax.shard_map(
        on_device,
        mesh=mesh,
        in_specs=placed,
        out_specs=(P("dp", "tp", "ctx"), P("dp", "tp", "ctx"), P(("tp", "ctx", "dp"), None)),
        check_vma=False,
    )
```

```python
import functools
import math

import jax
import jax.numpy as jnp
import ml_dtypes
import numpy as np
from jax import lax
from jax.experimental import pallas as pl
from jax.experimental.pallas import tpu as pltpu
from jax.sharding import PartitionSpec as P


def wave_table(rows, cols, length, sign):
    product = (
        jnp.arange(rows, dtype=jnp.int32)[:, None]
        * jnp.arange(cols, dtype=jnp.int32)[None, :]
        % length
    )
    angle = product.astype(jnp.float32) * (2.0 * math.pi / length)
    return (jnp.cos(angle), sign * jnp.sin(angle))


def mix_einsum(form, left, right):
    return jnp.einsum(form, left, right, precision=lax.Precision.HIGHEST)


def forward_spectrum(signal):
    chans, length = signal.shape
    total_len = 2 * length
    bits = total_len.bit_length() - 1
    outer_len = 2 ** (bits // 2)
    inner_len = total_len // outer_len
    half_outer = outer_len // 2
    folded = signal.reshape(chans, half_outer, inner_len)
    first_re, first_im = wave_table(outer_len, half_outer, outer_len, -1.0)
    mid_re = mix_einsum("kn,cna->cka", first_re, folded)
    mid_im = mix_einsum("kn,cna->cka", first_im, folded)
    twist_re, twist_im = wave_table(outer_len, inner_len, total_len, -1.0)
    rot_re = mid_re * twist_re - mid_im * twist_im
    rot_im = mid_re * twist_im + mid_im * twist_re
    last_re, last_im = wave_table(inner_len, inner_len, inner_len, -1.0)
    out_re = mix_einsum("cka,aj->ckj", rot_re, last_re) - mix_einsum("cka,aj->ckj", rot_im, last_im)
    out_im = mix_einsum("cka,aj->ckj", rot_re, last_im) + mix_einsum("cka,aj->ckj", rot_im, last_re)
    return (out_re, out_im)


def inverse_signal(spec_re, spec_im):
    chans, outer_len, inner_len = spec_re.shape
    total_len = outer_len * inner_len
    last_re, last_im = wave_table(inner_len, inner_len, inner_len, 1.0)
    mid_re = mix_einsum("ckj,ja->cka", spec_re, last_re) - mix_einsum(
        "ckj,ja->cka", spec_im, last_im
    )
    mid_im = mix_einsum("ckj,ja->cka", spec_re, last_im) + mix_einsum(
        "ckj,ja->cka", spec_im, last_re
    )
    twist_re, twist_im = wave_table(outer_len, inner_len, total_len, 1.0)
    rot_re = mid_re * twist_re - mid_im * twist_im
    rot_im = mid_re * twist_im + mid_im * twist_re
    first_re, first_im = wave_table(outer_len // 2, outer_len, outer_len, 1.0)
    signal = mix_einsum("nk,cka->cna", first_re, rot_re) - mix_einsum(
        "nk,cka->cna", first_im, rot_im
    )
    return signal.reshape(chans, -1) / total_len


def two_level_on_device(out_grad, gate_in, conv_in, filter_raw, out_weight):
    grad_rows = out_grad[0]
    gate_local = gate_in[0]
    conv_local = conv_in[0]
    unit_grad = lax.dot_general(
        out_weight,
        lax.all_gather(grad_rows, "tp", axis=0, tiled=True),
        (((1,), (1,)), ((), ())),
        preferred_element_type=jnp.float32,
    )
    gate_grad = (unit_grad * gate_local.astype(jnp.float32)).astype(jnp.bfloat16)
    gate_chan, conv_chan = (
        lax.all_to_all(gate_grad, "ctx", split_axis=0, concat_axis=1, tiled=True),
        lax.all_to_all(conv_local, "ctx", split_axis=0, concat_axis=1, tiled=True),
    )
    length = filter_raw.shape[1]
    norm_scale = 1.0 / math.sqrt(length)
    filt_re, filt_im = forward_spectrum(filter_raw * norm_scale)
    conv_re, conv_im = forward_spectrum(conv_chan.astype(jnp.float32))
    gate_re, gate_im = forward_spectrum(gate_chan.astype(jnp.float32))
    conv_out = inverse_signal(
        filt_re * conv_re - filt_im * conv_im, filt_re * conv_im + filt_im * conv_re
    ).astype(jnp.bfloat16)
    conv_grad = inverse_signal(
        filt_re * gate_re + filt_im * gate_im, filt_re * gate_im - filt_im * gate_re
    ).astype(jnp.bfloat16)
    cross_re = gate_re * conv_re + gate_im * conv_im
    cross_im = gate_im * conv_re - gate_re * conv_im
    back_out, back_grad = (
        lax.all_to_all(conv_out, "ctx", split_axis=1, concat_axis=0, tiled=True),
        lax.all_to_all(conv_grad, "ctx", split_axis=1, concat_axis=0, tiled=True),
    )
    gate_out = (unit_grad * back_out.astype(jnp.float32)).astype(jnp.bfloat16)
    summed_re, summed_im = (
        lax.psum_scatter(cross_re * norm_scale, "dp", scatter_dimension=0, tiled=True),
        lax.psum_scatter(cross_im * norm_scale, "dp", scatter_dimension=0, tiled=True),
    )
    filter_grad = inverse_signal(summed_re, summed_im)
    return (gate_out[None], back_grad[None], filter_grad)


TABLE_LIMIT_BYTES = 4 * 2**20
VMEM_BYTES = 24 * 2**20


def split_high_low(values):
    high = values.astype(ml_dtypes.bfloat16)
    low = (values - high.astype(np.float64)).astype(ml_dtypes.bfloat16)
    return high, low


@functools.lru_cache(maxsize=None)
def dense_tables(length):
    total = 2 * length
    time = np.arange(length)[:, None]
    freq = np.arange(length)[None, :]
    angle = (time * freq % total) * (2.0 * np.pi / total)
    even_odd = 1.0 - 2.0 * (np.arange(length) % 2)
    real, imag = np.cos(angle), -np.sin(angle)
    imag[:, 0] = even_odd
    weight = np.full((length, 1), 2.0 / total)
    weight[0] = 1.0 / total
    forward = np.concatenate([real, imag], axis=1)
    inverse = np.concatenate([real.T * weight, imag.T * weight], axis=0)
    return split_high_low(forward) + split_high_low(inverse)


def mm(left, right):
    return jnp.dot(left, right, preferred_element_type=jnp.float32)


def mm_nt(left, right):
    return lax.dot_general(left, right, (((1,), (1,)), ((), ())), preferred_element_type=jnp.float32)


def halves(values):
    high = values.astype(jnp.bfloat16)
    return high, (values - high.astype(jnp.float32)).astype(jnp.bfloat16)


def spectrum_product(left, right, conj_left):
    length = left.shape[1] // 2
    lr, li = left[:, :length], left[:, length:]
    rr, ri = right[:, :length], right[:, length:]
    ends = lax.broadcasted_iota(jnp.int32, lr.shape, 1) == 0
    both = li * ri
    if conj_left:
        real = lr * rr + jnp.where(ends, 0.0, both)
        imag = jnp.where(ends, both, lr * ri - li * rr)
    else:
        real = lr * rr - jnp.where(ends, 0.0, both)
        imag = jnp.where(ends, both, lr * ri + li * rr)
    return jnp.concatenate([real, imag], axis=1)


def inverse_dense(spec, inv_hi, inv_lo):
    high, low = halves(spec)
    return mm(high, inv_hi[...]) + mm(low, inv_hi[...]) + mm(high, inv_lo[...])


def place(index, size):
    return pl.ds(pl.multiple_of(index * size, size), size)


def offsets(parts):
    return [0, *reversed(range(1, parts))]


def middle_offsets(parts):
    return [0, *range(parts // 2, parts), *range(1, parts // 2)]


def gather_tokens(pieces, whole, here):
    step = pieces[0].shape[1]
    for k, piece in zip(offsets(len(pieces)), pieces):
        whole[:, place(here ^ k, step)] = piece[...]


def scatter_tokens(whole, pieces, here, order):
    step = pieces[0].shape[1]
    for k, piece in zip(order, pieces):
        piece[...] = whole[:, place(here ^ k, step)]


def blocks_kernel(source, *refs):
    out, sems = refs[:-1], refs[-1]
    here = lax.axis_index("ctx")
    rows = out[0].shape[0]
    copies = [
        pltpu.make_async_copy(source.at[place(here ^ k, rows), :], ref, sems.at[k - 1])
        for k, ref in zip(offsets(len(out) + 1)[1:], out)
    ]
    for copy in copies:
        copy.start()
    for copy in copies:
        copy.wait()


def filt_kernel(scale, filt, fwd_hi, fwd_lo, after_1, after_2, spec_filt):
    high, low = halves(filt[...] * scale)
    spec_filt[...] = mm(high, fwd_hi[...]) + mm(low, fwd_hi[...]) + mm(high, fwd_lo[...])


def spectrum_of(signal, fwd_hi, fwd_lo):
    return mm(signal, fwd_hi[...]) + mm(signal, fwd_lo[...])


def pair_rows(rows, mine):
    at = lax.axis_index("dp")
    return place(at if mine else 1 - at, rows)


def conv_kernel(parts, *refs):
    conv = refs[:parts]
    spec_filt, fwd_hi, fwd_lo, inv_hi, inv_lo = refs[parts : parts + 5]
    out = refs[parts + 5 : 2 * parts + 5]
    spec_conv, whole = refs[2 * parts + 5 :]
    here = lax.axis_index("ctx")
    step = conv[1].shape[1]
    whole[:, place(here, step)] = conv[0][place(here, whole.shape[0]), :]
    for k, piece in zip(offsets(parts)[1:], conv[1:]):
        whole[:, place(here ^ k, step)] = piece[...]
    spec_conv[...] = spectrum_of(whole[...], fwd_hi, fwd_lo)
    product = spectrum_product(spec_filt[...], spec_conv[...], False)
    whole[...] = inverse_dense(product, inv_hi, inv_lo).astype(jnp.bfloat16)
    scatter_tokens(whole, out, here, range(parts))


def unit_rows(order, weight, gate, rows_all, unit, out):
    here = lax.axis_index("ctx")
    for k, grad, ref in zip(order, unit, out):
        rows = grad.shape[0]
        at = place(here ^ k, rows)
        got = mm_nt(weight[at, :], rows_all[...])
        grad[...] = got
        ref[...] = (got * gate[at, :].astype(jnp.float32)).astype(jnp.bfloat16)


def far_unit_kernel(order, pieces, after, weight, gate, *refs):
    grads, count = refs[:pieces], len(order)
    unit, out, rows_all = refs[pieces : pieces + count], refs[pieces + count : -1], refs[-1]
    block = lax.axis_index("tp")
    rows = grads[0].shape[0]
    cut = grads[3].shape[1]
    for k, ref in enumerate(grads[:3]):
        rows_all[place(block ^ k, rows), :] = ref[...]
    rows_all[place(block ^ 3, rows), :cut] = grads[3][...]
    rows_all[place(block ^ 3, rows), cut:] = grads[4][...]
    unit_rows(order, weight, gate, rows_all, unit, out)


def own_unit_kernel(order, weight, gate, rows_all, unit, out):
    unit_rows(order, weight, gate, rows_all, [unit], [out])


def grad_kernel(parts, *refs):
    gate = refs[:parts]
    spec_filt, fwd_hi, fwd_lo, inv_hi, inv_lo = refs[parts : parts + 5]
    out = refs[parts + 5 : 2 * parts + 5]
    spec_gate, whole = refs[2 * parts + 5 :]
    here = lax.axis_index("ctx")
    gather_tokens(gate, whole, here)
    spec_gate[...] = spectrum_of(whole[...], fwd_hi, fwd_lo)
    product = spectrum_product(spec_filt[...], spec_gate[...], True)
    whole[...] = inverse_dense(product, inv_hi, inv_lo).astype(jnp.bfloat16)
    scatter_tokens(whole, out, here, middle_offsets(parts))


def filter_kernel(parts, scale, spec_conv, spec_gate, inv_hi, inv_lo, *refs):
    keep, *send, whole = refs[parts:]
    product = spectrum_product(spec_conv[...], spec_gate[...], True)
    whole[...] = inverse_dense(product, inv_hi, inv_lo) * scale
    rows = keep.shape[0]
    keep[...] = whole[pair_rows(rows, True), :]
    for i, ref in enumerate(send):
        step = ref.shape[0]
        at = pl.multiple_of(pair_rows(rows, False).start + i * step, step)
        ref[...] = whole[pl.ds(at, step), :].astype(jnp.bfloat16)


def gate_kernel(parts, *refs):
    unit, back, out = refs[:parts], refs[parts : 2 * parts], refs[2 * parts]
    here = lax.axis_index("ctx")
    rows = back[0].shape[0]
    for k, grad, ref in zip(range(parts), unit, back):
        gated = grad[...] * ref[...].astype(jnp.float32)
        out[place(here ^ k, rows), :] = gated.astype(jnp.bfloat16)


def last_kernel(parts, *refs):
    back, (low, high, keep, total, out) = refs[:parts], refs[parts:]
    step = low.shape[0]
    for i, ref in enumerate((low, high)):
        at = slice(i * step, (i + 1) * step)
        total[at, :] = keep[at, :] + ref[...].astype(jnp.float32)
    here = lax.axis_index("ctx")
    rows = back[0].shape[0]
    for k, ref in zip(middle_offsets(parts), back):
        out[place(here ^ k, rows), :] = ref[...]


def call(kernel, outs, args, scratch=(), far=(), cost=1.0):
    vmem = pl.BlockSpec(memory_space=pltpu.VMEM)
    hbm = pl.BlockSpec(memory_space=pltpu.HBM)
    held = [
        pltpu.with_memory_space_constraint(a, pltpu.HBM) if i in far else a
        for i, a in enumerate(args)
    ]
    return pl.pallas_call(
        kernel,
        out_shape=outs,
        in_specs=[hbm if i in far else vmem for i in range(len(args))],
        out_specs=jax.tree.map(lambda _: vmem, outs),
        scratch_shapes=list(scratch),
        cost_estimate=pl.CostEstimate(
            flops=int(cost * 1e9), bytes_accessed=int(cost * 1e6), transcendentals=0
        ),
        compiler_params=pltpu.CompilerParams(vmem_limit_bytes=VMEM_BYTES),
    )(*held)


def dense_on_device(parts, groups, out_grad, gate_in, conv_in, filter_raw, out_weight):
    f32, bf16 = jnp.float32, jnp.bfloat16
    grad_rows, gate_local, conv_local = out_grad[0], gate_in[0], conv_in[0]
    chans, length = filter_raw.shape
    channels, tokens = conv_local.shape
    width = grad_rows.shape[1]
    scale = 1.0 / math.sqrt(length)
    tables = [jnp.asarray(t) for t in dense_tables(length)]
    shape = jax.ShapeDtypeStruct

    def swap(value, axis, size, k):
        return lax.ppermute(value, axis, [(i, i ^ k) for i in range(size)])

    def exchange(pieces, order):
        return [swap(p, "ctx", parts, k) if k else p for k, p in zip(order, pieces)]

    grad_1 = swap(grad_rows, "tp", groups, 1)
    grad_2 = swap(grad_rows, "tp", groups, 2)
    blocks = call(
        blocks_kernel,
        [shape((chans, tokens), bf16)] * (parts - 1),
        [conv_local],
        [pltpu.SemaphoreType.DMA((parts - 1,))],
        far=(0,),
        cost=10.0,
    )
    conv_pieces = exchange(blocks, offsets(parts)[1:])
    cut = width // 32 * 11
    grad_3a = swap(grad_1[:, :cut], "tp", groups, 2)
    grad_3b = swap(grad_2[:, cut:], "tp", groups, 1)

    piece = shape((chans, tokens), bf16)
    spectrum = shape((chans, 2 * length), f32)
    whole = pltpu.VMEM((chans, length), bf16)
    spec_filt = call(
        functools.partial(filt_kernel, scale),
        spectrum,
        [filter_raw, *tables[:2], grad_1, grad_2],
        cost=2.0,
    )
    *conv_out, spec_conv = call(
        functools.partial(conv_kernel, parts),
        [piece] * parts + [spectrum],
        [conv_local, *conv_pieces, spec_filt, *tables],
        [whole],
        cost=2.0,
    )

    away = offsets(parts)[1:]
    grad_all = shape((groups * grad_rows.shape[0], width), bf16)
    unit_piece = shape((chans, tokens), f32)
    *far, grad_all = call(
        functools.partial(far_unit_kernel, away, 5),
        [unit_piece] * len(away) + [piece] * len(away) + [grad_all],
        [conv_out[0], out_weight, gate_local, grad_rows, grad_1, grad_2, grad_3a, grad_3b],
    )
    unit_own, gate_own = call(
        functools.partial(own_unit_kernel, [0]),
        [unit_piece, piece],
        [out_weight, gate_local, grad_all],
    )
    *conv_out, gate_own = lax.optimization_barrier((*conv_out, gate_own))
    conv_back = exchange(conv_out, range(parts))
    gate_chan = exchange([gate_own, *far[len(away) :]], offsets(parts))
    unit = dict(zip(offsets(parts), [unit_own, *far[: len(away)]]))
    *conv_grad, spec_gate = call(
        functools.partial(grad_kernel, parts),
        [piece] * parts + [spectrum],
        [*gate_chan, spec_filt, *tables],
        [whole],
    )
    grad_back = exchange(conv_grad, middle_offsets(parts))
    half, local = shape((chans // 2, length), f32), shape((channels, tokens), bf16)
    quarter = shape((chans // 4, length), bf16)
    gate_out = call(
        functools.partial(gate_kernel, parts),
        local,
        [*(unit[k] for k in range(parts)), *conv_back],
    )
    keep, send_low, send_high = call(
        functools.partial(filter_kernel, parts, scale),
        [half, quarter, quarter],
        [spec_conv, spec_gate, *tables[2:], *conv_back],
        [pltpu.VMEM((chans, length), f32)],
        cost=2.0,
    )
    filter_grad, conv_grad_out = call(
        functools.partial(last_kernel, parts),
        [half, local],
        [*grad_back, swap(send_low, "dp", 2, 1), swap(send_high, "dp", 2, 1), keep],
    )
    return (gate_out[None], conv_grad_out[None], filter_grad)


def solution(mesh):
    placed = (
        P("dp", ("ctx", "tp"), None),
        P("dp", "tp", "ctx"),
        P("dp", "tp", "ctx"),
        P(("tp", "ctx"), None),
        P("tp", None),
    )
    parts, groups, pair = mesh.shape["ctx"], mesh.shape["tp"], mesh.shape["dp"]

    def on_device(out_grad, gate_in, conv_in, filter_raw, out_weight):
        args = (out_grad, gate_in, conv_in, filter_raw, out_weight)
        table = 4 * filter_raw.shape[1] ** 2 * jnp.dtype(jnp.bfloat16).itemsize
        one_sequence = out_grad.shape[0] == 1
        power = parts & (parts - 1) == 0
        if one_sequence and power and parts > 1 and groups == 4 and pair == 2 and table <= TABLE_LIMIT_BYTES:
            return dense_on_device(parts, groups, *args)
        return two_level_on_device(*args)

    return jax.shard_map(
        on_device,
        mesh=mesh,
        in_specs=placed,
        out_specs=(P("dp", "tp", "ctx"), P("dp", "tp", "ctx"), P(("tp", "ctx", "dp"), None)),
        check_vma=False,
    )
```

```python
import functools
import math

import jax
import jax.numpy as jnp
import ml_dtypes
import numpy as np
from jax import lax
from jax.experimental import pallas as pl
from jax.experimental.pallas import tpu as pltpu
from jax.sharding import PartitionSpec as P


def wave_table(rows, cols, length, sign):
    product = (
        jnp.arange(rows, dtype=jnp.int32)[:, None]
        * jnp.arange(cols, dtype=jnp.int32)[None, :]
        % length
    )
    angle = product.astype(jnp.float32) * (2.0 * math.pi / length)
    return (jnp.cos(angle), sign * jnp.sin(angle))


def mix_einsum(form, left, right):
    return jnp.einsum(form, left, right, precision=lax.Precision.HIGHEST)


def forward_spectrum(signal):
    chans, length = signal.shape
    total_len = 2 * length
    bits = total_len.bit_length() - 1
    outer_len = 2 ** (bits // 2)
    inner_len = total_len // outer_len
    half_outer = outer_len // 2
    folded = signal.reshape(chans, half_outer, inner_len)
    first_re, first_im = wave_table(outer_len, half_outer, outer_len, -1.0)
    mid_re = mix_einsum("kn,cna->cka", first_re, folded)
    mid_im = mix_einsum("kn,cna->cka", first_im, folded)
    twist_re, twist_im = wave_table(outer_len, inner_len, total_len, -1.0)
    rot_re = mid_re * twist_re - mid_im * twist_im
    rot_im = mid_re * twist_im + mid_im * twist_re
    last_re, last_im = wave_table(inner_len, inner_len, inner_len, -1.0)
    out_re = mix_einsum("cka,aj->ckj", rot_re, last_re) - mix_einsum("cka,aj->ckj", rot_im, last_im)
    out_im = mix_einsum("cka,aj->ckj", rot_re, last_im) + mix_einsum("cka,aj->ckj", rot_im, last_re)
    return (out_re, out_im)


def inverse_signal(spec_re, spec_im):
    chans, outer_len, inner_len = spec_re.shape
    total_len = outer_len * inner_len
    last_re, last_im = wave_table(inner_len, inner_len, inner_len, 1.0)
    mid_re = mix_einsum("ckj,ja->cka", spec_re, last_re) - mix_einsum(
        "ckj,ja->cka", spec_im, last_im
    )
    mid_im = mix_einsum("ckj,ja->cka", spec_re, last_im) + mix_einsum(
        "ckj,ja->cka", spec_im, last_re
    )
    twist_re, twist_im = wave_table(outer_len, inner_len, total_len, 1.0)
    rot_re = mid_re * twist_re - mid_im * twist_im
    rot_im = mid_re * twist_im + mid_im * twist_re
    first_re, first_im = wave_table(outer_len // 2, outer_len, outer_len, 1.0)
    signal = mix_einsum("nk,cka->cna", first_re, rot_re) - mix_einsum(
        "nk,cka->cna", first_im, rot_im
    )
    return signal.reshape(chans, -1) / total_len


def two_level_on_device(out_grad, gate_in, conv_in, filter_raw, out_weight):
    grad_rows = out_grad[0]
    gate_local = gate_in[0]
    conv_local = conv_in[0]
    unit_grad = lax.dot_general(
        out_weight,
        lax.all_gather(grad_rows, "tp", axis=0, tiled=True),
        (((1,), (1,)), ((), ())),
        preferred_element_type=jnp.float32,
    )
    gate_grad = (unit_grad * gate_local.astype(jnp.float32)).astype(jnp.bfloat16)
    gate_chan, conv_chan = (
        lax.all_to_all(gate_grad, "ctx", split_axis=0, concat_axis=1, tiled=True),
        lax.all_to_all(conv_local, "ctx", split_axis=0, concat_axis=1, tiled=True),
    )
    length = filter_raw.shape[1]
    norm_scale = 1.0 / math.sqrt(length)
    filt_re, filt_im = forward_spectrum(filter_raw * norm_scale)
    conv_re, conv_im = forward_spectrum(conv_chan.astype(jnp.float32))
    gate_re, gate_im = forward_spectrum(gate_chan.astype(jnp.float32))
    conv_out = inverse_signal(
        filt_re * conv_re - filt_im * conv_im, filt_re * conv_im + filt_im * conv_re
    ).astype(jnp.bfloat16)
    conv_grad = inverse_signal(
        filt_re * gate_re + filt_im * gate_im, filt_re * gate_im - filt_im * gate_re
    ).astype(jnp.bfloat16)
    cross_re = gate_re * conv_re + gate_im * conv_im
    cross_im = gate_im * conv_re - gate_re * conv_im
    back_out, back_grad = (
        lax.all_to_all(conv_out, "ctx", split_axis=1, concat_axis=0, tiled=True),
        lax.all_to_all(conv_grad, "ctx", split_axis=1, concat_axis=0, tiled=True),
    )
    gate_out = (unit_grad * back_out.astype(jnp.float32)).astype(jnp.bfloat16)
    summed_re, summed_im = (
        lax.psum_scatter(cross_re * norm_scale, "dp", scatter_dimension=0, tiled=True),
        lax.psum_scatter(cross_im * norm_scale, "dp", scatter_dimension=0, tiled=True),
    )
    filter_grad = inverse_signal(summed_re, summed_im)
    return (gate_out[None], back_grad[None], filter_grad)


TABLE_LIMIT_BYTES = 4 * 2**20
VMEM_BYTES = 24 * 2**20


def split_high_low(values):
    high = values.astype(ml_dtypes.bfloat16)
    low = (values - high.astype(np.float64)).astype(ml_dtypes.bfloat16)
    return high, low


@functools.lru_cache(maxsize=None)
def dense_tables(length):
    total = 2 * length
    time = np.arange(length)[:, None]
    freq = np.arange(length)[None, :]
    angle = (time * freq % total) * (2.0 * np.pi / total)
    even_odd = 1.0 - 2.0 * (np.arange(length) % 2)
    real, imag = np.cos(angle), -np.sin(angle)
    imag[:, 0] = even_odd
    weight = np.full((length, 1), 2.0 / total)
    weight[0] = 1.0 / total
    forward = np.concatenate([real, imag], axis=1)
    inverse = np.concatenate([real.T * weight, imag.T * weight], axis=0)
    return split_high_low(forward) + split_high_low(inverse)


def mm(left, right):
    return jnp.dot(left, right, preferred_element_type=jnp.float32)


def mm_nt(left, right):
    return lax.dot_general(left, right, (((1,), (1,)), ((), ())), preferred_element_type=jnp.float32)


def halves(values):
    high = values.astype(jnp.bfloat16)
    return high, (values - high.astype(jnp.float32)).astype(jnp.bfloat16)


def spectrum_product(left, right, conj_left):
    length = left.shape[1] // 2
    lr, li = left[:, :length], left[:, length:]
    rr, ri = right[:, :length], right[:, length:]
    ends = lax.broadcasted_iota(jnp.int32, lr.shape, 1) == 0
    both = li * ri
    if conj_left:
        real = lr * rr + jnp.where(ends, 0.0, both)
        imag = jnp.where(ends, both, lr * ri - li * rr)
    else:
        real = lr * rr - jnp.where(ends, 0.0, both)
        imag = jnp.where(ends, both, lr * ri + li * rr)
    return jnp.concatenate([real, imag], axis=1)


def inverse_dense(spec, inv_hi, inv_lo):
    high, low = halves(spec)
    return mm(high, inv_hi[...]) + mm(low, inv_hi[...]) + mm(high, inv_lo[...])


def place(index, size):
    return pl.ds(pl.multiple_of(index * size, size), size)


def offsets(parts):
    return [0, *reversed(range(1, parts))]


def middle_offsets(parts):
    return [0, *range(parts // 2, parts), *range(1, parts // 2)]


def gather_tokens(pieces, whole, here):
    step = pieces[0].shape[1]
    for k, piece in zip(offsets(len(pieces)), pieces):
        whole[:, place(here ^ k, step)] = piece[...]


def scatter_tokens(whole, pieces, here, order):
    step = pieces[0].shape[1]
    for k, piece in zip(order, pieces):
        piece[...] = whole[:, place(here ^ k, step)]


def blocks_kernel(source, *refs):
    out, sems = refs[:-1], refs[-1]
    here = lax.axis_index("ctx")
    rows = out[0].shape[0]
    copies = [
        pltpu.make_async_copy(source.at[place(here ^ k, rows), :], ref, sems.at[k - 1])
        for k, ref in zip(offsets(len(out) + 1)[1:], out)
    ]
    for copy in copies:
        copy.start()
    for copy in copies:
        copy.wait()


def filt_kernel(scale, filt, fwd_hi, fwd_lo, after_1, after_2, spec_filt):
    high, low = halves(filt[...] * scale)
    spec_filt[...] = mm(high, fwd_hi[...]) + mm(low, fwd_hi[...]) + mm(high, fwd_lo[...])


def spectrum_of(signal, fwd_hi, fwd_lo):
    return mm(signal, fwd_hi[...]) + mm(signal, fwd_lo[...])


def pair_rows(rows, mine):
    at = lax.axis_index("dp")
    return place(at if mine else 1 - at, rows)


def conv_kernel(parts, *refs):
    conv = refs[:parts]
    spec_filt, fwd_hi, fwd_lo, inv_hi, inv_lo = refs[parts : parts + 5]
    out = refs[parts + 5 : 2 * parts + 5]
    spec_conv, whole = refs[2 * parts + 5 :]
    here = lax.axis_index("ctx")
    step = conv[1].shape[1]
    whole[:, place(here, step)] = conv[0][place(here, whole.shape[0]), :]
    for k, piece in zip(offsets(parts)[1:], conv[1:]):
        whole[:, place(here ^ k, step)] = piece[...]
    spec_conv[...] = spectrum_of(whole[...], fwd_hi, fwd_lo)
    product = spectrum_product(spec_filt[...], spec_conv[...], False)
    whole[...] = inverse_dense(product, inv_hi, inv_lo).astype(jnp.bfloat16)
    scatter_tokens(whole, out, here, range(parts))


def unit_rows(order, weight, gate, rows_all, unit, out):
    here = lax.axis_index("ctx")
    for k, grad, ref in zip(order, unit, out):
        rows = grad.shape[0]
        at = place(here ^ k, rows)
        got = mm_nt(weight[at, :], rows_all[...])
        grad[...] = got
        ref[...] = (got * gate[at, :].astype(jnp.float32)).astype(jnp.bfloat16)


def far_unit_kernel(order, pieces, after, weight, gate, *refs):
    grads, count = refs[:pieces], len(order)
    unit, out, rows_all = refs[pieces : pieces + count], refs[pieces + count : -1], refs[-1]
    block = lax.axis_index("tp")
    rows = grads[0].shape[0]
    cut = grads[3].shape[1]
    for k, ref in enumerate(grads[:3]):
        rows_all[place(block ^ k, rows), :] = ref[...]
    rows_all[place(block ^ 3, rows), :cut] = grads[3][...]
    rows_all[place(block ^ 3, rows), cut:] = grads[4][...]
    unit_rows(order, weight, gate, rows_all, unit, out)


def own_unit_kernel(order, weight, gate, rows_all, unit, out):
    unit_rows(order, weight, gate, rows_all, [unit], [out])


def grad_kernel(parts, *refs):
    gate = refs[:parts]
    spec_filt, fwd_hi, fwd_lo, inv_hi, inv_lo = refs[parts : parts + 5]
    out = refs[parts + 5 : 2 * parts + 5]
    spec_gate, whole = refs[2 * parts + 5 :]
    here = lax.axis_index("ctx")
    gather_tokens(gate, whole, here)
    spec_gate[...] = spectrum_of(whole[...], fwd_hi, fwd_lo)
    product = spectrum_product(spec_filt[...], spec_gate[...], True)
    whole[...] = inverse_dense(product, inv_hi, inv_lo).astype(jnp.bfloat16)
    scatter_tokens(whole, out, here, middle_offsets(parts))


def filter_kernel(parts, scale, spec_conv, spec_gate, inv_hi, inv_lo, *refs):
    keep, *send, whole = refs[parts - 2 :]
    product = spectrum_product(spec_conv[...], spec_gate[...], True)
    whole[...] = inverse_dense(product, inv_hi, inv_lo) * scale
    rows = keep.shape[0]
    keep[...] = whole[pair_rows(rows, True), :]
    for i, ref in enumerate(send):
        step = ref.shape[0]
        at = pl.multiple_of(pair_rows(rows, False).start + i * step, step)
        ref[...] = whole[pl.ds(at, step), :].astype(jnp.bfloat16)


def gate_kernel(parts, *refs):
    unit, back, out = refs[:parts], refs[parts : 2 * parts], refs[2 * parts]
    here = lax.axis_index("ctx")
    rows = back[0].shape[0]
    for k, grad, ref in zip(range(parts), unit, back):
        gated = grad[...] * ref[...].astype(jnp.float32)
        out[place(here ^ k, rows), :] = gated.astype(jnp.bfloat16)


def last_kernel(parts, *refs):
    back, (low, high, keep, total, out) = refs[:parts], refs[parts:]
    step = low.shape[0]
    for i, ref in enumerate((low, high)):
        at = slice(i * step, (i + 1) * step)
        total[at, :] = keep[at, :] + ref[...].astype(jnp.float32)
    here = lax.axis_index("ctx")
    rows = back[0].shape[0]
    for k, ref in zip(middle_offsets(parts), back):
        out[place(here ^ k, rows), :] = ref[...]


def call(kernel, outs, args, scratch=(), far=(), cost=1.0):
    vmem = pl.BlockSpec(memory_space=pltpu.VMEM)
    hbm = pl.BlockSpec(memory_space=pltpu.HBM)
    held = [
        pltpu.with_memory_space_constraint(a, pltpu.HBM) if i in far else a
        for i, a in enumerate(args)
    ]
    return pl.pallas_call(
        kernel,
        out_shape=outs,
        in_specs=[hbm if i in far else vmem for i in range(len(args))],
        out_specs=jax.tree.map(lambda _: vmem, outs),
        scratch_shapes=list(scratch),
        cost_estimate=pl.CostEstimate(
            flops=int(cost * 1e9), bytes_accessed=int(cost * 1e6), transcendentals=0
        ),
        compiler_params=pltpu.CompilerParams(vmem_limit_bytes=VMEM_BYTES),
    )(*held)


def dense_on_device(parts, groups, out_grad, gate_in, conv_in, filter_raw, out_weight):
    f32, bf16 = jnp.float32, jnp.bfloat16
    grad_rows, gate_local, conv_local = out_grad[0], gate_in[0], conv_in[0]
    chans, length = filter_raw.shape
    channels, tokens = conv_local.shape
    width = grad_rows.shape[1]
    scale = 1.0 / math.sqrt(length)
    tables = [jnp.asarray(t) for t in dense_tables(length)]
    shape = jax.ShapeDtypeStruct

    def swap(value, axis, size, k):
        return lax.ppermute(value, axis, [(i, i ^ k) for i in range(size)])

    def exchange(pieces, order):
        return [swap(p, "ctx", parts, k) if k else p for k, p in zip(order, pieces)]

    grad_1 = swap(grad_rows, "tp", groups, 1)
    grad_2 = swap(grad_rows, "tp", groups, 2)
    blocks = call(
        blocks_kernel,
        [shape((chans, tokens), bf16)] * (parts - 1),
        [conv_local],
        [pltpu.SemaphoreType.DMA((parts - 1,))],
        far=(0,),
        cost=10.0,
    )
    conv_pieces = exchange(blocks, offsets(parts)[1:])
    cut = width // 32 * 11
    grad_3a = swap(grad_1[:, :cut], "tp", groups, 2)
    grad_3b = swap(grad_2[:, cut:], "tp", groups, 1)

    piece = shape((chans, tokens), bf16)
    spectrum = shape((chans, 2 * length), f32)
    whole = pltpu.VMEM((chans, length), bf16)
    spec_filt = call(
        functools.partial(filt_kernel, scale),
        spectrum,
        [filter_raw, *tables[:2], grad_1, grad_2],
        cost=2.0,
    )
    *conv_out, spec_conv = call(
        functools.partial(conv_kernel, parts),
        [piece] * parts + [spectrum],
        [conv_local, *conv_pieces, spec_filt, *tables],
        [whole],
        cost=2.0,
    )

    away = offsets(parts)[1:]
    grad_all = shape((groups * grad_rows.shape[0], width), bf16)
    unit_piece = shape((chans, tokens), f32)
    *far, grad_all = call(
        functools.partial(far_unit_kernel, away, 5),
        [unit_piece] * len(away) + [piece] * len(away) + [grad_all],
        [conv_out[0], out_weight, gate_local, grad_rows, grad_1, grad_2, grad_3a, grad_3b],
    )
    unit_own, gate_own = call(
        functools.partial(own_unit_kernel, [0]),
        [unit_piece, piece],
        [out_weight, gate_local, grad_all],
    )
    *conv_out, gate_own = lax.optimization_barrier((*conv_out, gate_own))
    conv_back = exchange(conv_out, range(parts))
    gate_chan = exchange([gate_own, *far[len(away) :]], offsets(parts))
    unit = dict(zip(offsets(parts), [unit_own, *far[: len(away)]]))
    *conv_grad, spec_gate = call(
        functools.partial(grad_kernel, parts),
        [piece] * parts + [spectrum],
        [*gate_chan, spec_filt, *tables],
        [whole],
    )
    grad_back = exchange(conv_grad, middle_offsets(parts))
    half, local = shape((chans // 2, length), f32), shape((channels, tokens), bf16)
    quarter = shape((chans // 4, length), bf16)
    gate_out = call(
        functools.partial(gate_kernel, parts),
        local,
        [*(unit[k] for k in range(parts)), *conv_back],
    )
    keep, send_low, send_high = call(
        functools.partial(filter_kernel, parts, scale),
        [half, quarter, quarter],
        [spec_conv, spec_gate, *tables[2:], *conv_back[1:-1]],
        [pltpu.VMEM((chans, length), f32)],
        cost=2.0,
    )
    filter_grad, conv_grad_out = call(
        functools.partial(last_kernel, parts),
        [half, local],
        [*grad_back, swap(send_low, "dp", 2, 1), swap(send_high, "dp", 2, 1), keep],
    )
    return (gate_out[None], conv_grad_out[None], filter_grad)


def solution(mesh):
    placed = (
        P("dp", ("ctx", "tp"), None),
        P("dp", "tp", "ctx"),
        P("dp", "tp", "ctx"),
        P(("tp", "ctx"), None),
        P("tp", None),
    )
    parts, groups, pair = mesh.shape["ctx"], mesh.shape["tp"], mesh.shape["dp"]

    def on_device(out_grad, gate_in, conv_in, filter_raw, out_weight):
        args = (out_grad, gate_in, conv_in, filter_raw, out_weight)
        table = 4 * filter_raw.shape[1] ** 2 * jnp.dtype(jnp.bfloat16).itemsize
        one_sequence = out_grad.shape[0] == 1
        power = parts & (parts - 1) == 0
        if one_sequence and power and parts > 1 and groups == 4 and pair == 2 and table <= TABLE_LIMIT_BYTES:
            return dense_on_device(parts, groups, *args)
        return two_level_on_device(*args)

    return jax.shard_map(
        on_device,
        mesh=mesh,
        in_specs=placed,
        out_specs=(P("dp", "tp", "ctx"), P("dp", "tp", "ctx"), P(("tp", "ctx", "dp"), None)),
        check_vma=False,
    )
```

```python
import functools
import math

import jax
import jax.numpy as jnp
import ml_dtypes
import numpy as np
from jax import lax
from jax.experimental import pallas as pl
from jax.experimental.pallas import tpu as pltpu
from jax.sharding import PartitionSpec as P


def wave_table(rows, cols, length, sign):
    product = (
        jnp.arange(rows, dtype=jnp.int32)[:, None]
        * jnp.arange(cols, dtype=jnp.int32)[None, :]
        % length
    )
    angle = product.astype(jnp.float32) * (2.0 * math.pi / length)
    return (jnp.cos(angle), sign * jnp.sin(angle))


def mix_einsum(form, left, right):
    return jnp.einsum(form, left, right, precision=lax.Precision.HIGHEST)


def forward_spectrum(signal):
    chans, length = signal.shape
    total_len = 2 * length
    bits = total_len.bit_length() - 1
    outer_len = 2 ** (bits // 2)
    inner_len = total_len // outer_len
    half_outer = outer_len // 2
    folded = signal.reshape(chans, half_outer, inner_len)
    first_re, first_im = wave_table(outer_len, half_outer, outer_len, -1.0)
    mid_re = mix_einsum("kn,cna->cka", first_re, folded)
    mid_im = mix_einsum("kn,cna->cka", first_im, folded)
    twist_re, twist_im = wave_table(outer_len, inner_len, total_len, -1.0)
    rot_re = mid_re * twist_re - mid_im * twist_im
    rot_im = mid_re * twist_im + mid_im * twist_re
    last_re, last_im = wave_table(inner_len, inner_len, inner_len, -1.0)
    out_re = mix_einsum("cka,aj->ckj", rot_re, last_re) - mix_einsum("cka,aj->ckj", rot_im, last_im)
    out_im = mix_einsum("cka,aj->ckj", rot_re, last_im) + mix_einsum("cka,aj->ckj", rot_im, last_re)
    return (out_re, out_im)


def inverse_signal(spec_re, spec_im):
    chans, outer_len, inner_len = spec_re.shape
    total_len = outer_len * inner_len
    last_re, last_im = wave_table(inner_len, inner_len, inner_len, 1.0)
    mid_re = mix_einsum("ckj,ja->cka", spec_re, last_re) - mix_einsum(
        "ckj,ja->cka", spec_im, last_im
    )
    mid_im = mix_einsum("ckj,ja->cka", spec_re, last_im) + mix_einsum(
        "ckj,ja->cka", spec_im, last_re
    )
    twist_re, twist_im = wave_table(outer_len, inner_len, total_len, 1.0)
    rot_re = mid_re * twist_re - mid_im * twist_im
    rot_im = mid_re * twist_im + mid_im * twist_re
    first_re, first_im = wave_table(outer_len // 2, outer_len, outer_len, 1.0)
    signal = mix_einsum("nk,cka->cna", first_re, rot_re) - mix_einsum(
        "nk,cka->cna", first_im, rot_im
    )
    return signal.reshape(chans, -1) / total_len


def two_level_on_device(out_grad, gate_in, conv_in, filter_raw, out_weight):
    grad_rows = out_grad[0]
    gate_local = gate_in[0]
    conv_local = conv_in[0]
    unit_grad = lax.dot_general(
        out_weight,
        lax.all_gather(grad_rows, "tp", axis=0, tiled=True),
        (((1,), (1,)), ((), ())),
        preferred_element_type=jnp.float32,
    )
    gate_grad = (unit_grad * gate_local.astype(jnp.float32)).astype(jnp.bfloat16)
    gate_chan, conv_chan = (
        lax.all_to_all(gate_grad, "ctx", split_axis=0, concat_axis=1, tiled=True),
        lax.all_to_all(conv_local, "ctx", split_axis=0, concat_axis=1, tiled=True),
    )
    length = filter_raw.shape[1]
    norm_scale = 1.0 / math.sqrt(length)
    filt_re, filt_im = forward_spectrum(filter_raw * norm_scale)
    conv_re, conv_im = forward_spectrum(conv_chan.astype(jnp.float32))
    gate_re, gate_im = forward_spectrum(gate_chan.astype(jnp.float32))
    conv_out = inverse_signal(
        filt_re * conv_re - filt_im * conv_im, filt_re * conv_im + filt_im * conv_re
    ).astype(jnp.bfloat16)
    conv_grad = inverse_signal(
        filt_re * gate_re + filt_im * gate_im, filt_re * gate_im - filt_im * gate_re
    ).astype(jnp.bfloat16)
    cross_re = gate_re * conv_re + gate_im * conv_im
    cross_im = gate_im * conv_re - gate_re * conv_im
    back_out, back_grad = (
        lax.all_to_all(conv_out, "ctx", split_axis=1, concat_axis=0, tiled=True),
        lax.all_to_all(conv_grad, "ctx", split_axis=1, concat_axis=0, tiled=True),
    )
    gate_out = (unit_grad * back_out.astype(jnp.float32)).astype(jnp.bfloat16)
    summed_re, summed_im = (
        lax.psum_scatter(cross_re * norm_scale, "dp", scatter_dimension=0, tiled=True),
        lax.psum_scatter(cross_im * norm_scale, "dp", scatter_dimension=0, tiled=True),
    )
    filter_grad = inverse_signal(summed_re, summed_im)
    return (gate_out[None], back_grad[None], filter_grad)


TABLE_LIMIT_BYTES = 4 * 2**20
VMEM_BYTES = 24 * 2**20


def split_high_low(values):
    high = values.astype(ml_dtypes.bfloat16)
    low = (values - high.astype(np.float64)).astype(ml_dtypes.bfloat16)
    return high, low


@functools.lru_cache(maxsize=None)
def dense_tables(length):
    total = 2 * length
    time = np.arange(length)[:, None]
    freq = np.arange(length)[None, :]
    angle = (time * freq % total) * (2.0 * np.pi / total)
    even_odd = 1.0 - 2.0 * (np.arange(length) % 2)
    real, imag = np.cos(angle), -np.sin(angle)
    imag[:, 0] = even_odd
    weight = np.full((length, 1), 2.0 / total)
    weight[0] = 1.0 / total
    forward = np.concatenate([real, imag], axis=1)
    inverse = np.concatenate([real.T * weight, imag.T * weight], axis=0)
    return split_high_low(forward) + split_high_low(inverse)


def mm(left, right):
    return jnp.dot(left, right, preferred_element_type=jnp.float32)


def mm_nt(left, right):
    return lax.dot_general(left, right, (((1,), (1,)), ((), ())), preferred_element_type=jnp.float32)


def halves(values):
    high = values.astype(jnp.bfloat16)
    return high, (values - high.astype(jnp.float32)).astype(jnp.bfloat16)


def spectrum_product(left, right, conj_left):
    length = left.shape[1] // 2
    lr, li = left[:, :length], left[:, length:]
    rr, ri = right[:, :length], right[:, length:]
    ends = lax.broadcasted_iota(jnp.int32, lr.shape, 1) == 0
    both = li * ri
    if conj_left:
        real = lr * rr + jnp.where(ends, 0.0, both)
        imag = jnp.where(ends, both, lr * ri - li * rr)
    else:
        real = lr * rr - jnp.where(ends, 0.0, both)
        imag = jnp.where(ends, both, lr * ri + li * rr)
    return jnp.concatenate([real, imag], axis=1)


def inverse_dense(spec, inv_hi, inv_lo):
    high, low = halves(spec)
    return mm(high, inv_hi[...]) + mm(low, inv_hi[...]) + mm(high, inv_lo[...])


def place(index, size):
    return pl.ds(pl.multiple_of(index * size, size), size)


def offsets(parts):
    return [0, *reversed(range(1, parts))]


def middle_offsets(parts):
    return [0, *range(parts // 2, parts), *range(1, parts // 2)]


def gather_tokens(pieces, whole, here):
    step = pieces[0].shape[1]
    for k, piece in zip(offsets(len(pieces)), pieces):
        whole[:, place(here ^ k, step)] = piece[...]


def scatter_tokens(whole, pieces, here, order):
    step = pieces[0].shape[1]
    for k, piece in zip(order, pieces):
        piece[...] = whole[:, place(here ^ k, step)]


def blocks_kernel(source, *refs):
    out, sems = refs[:-1], refs[-1]
    here = lax.axis_index("ctx")
    rows = out[0].shape[0]
    copies = [
        pltpu.make_async_copy(source.at[place(here ^ k, rows), :], ref, sems.at[k - 1])
        for k, ref in zip(offsets(len(out) + 1)[1:], out)
    ]
    for copy in copies:
        copy.start()
    for copy in copies:
        copy.wait()


def filt_kernel(scale, filt, fwd_hi, fwd_lo, after_1, after_2, spec_filt):
    high, low = halves(filt[...] * scale)
    spec_filt[...] = mm(high, fwd_hi[...]) + mm(low, fwd_hi[...]) + mm(high, fwd_lo[...])


def spectrum_of(signal, fwd_hi, fwd_lo):
    return mm(signal, fwd_hi[...]) + mm(signal, fwd_lo[...])


def pair_rows(rows, mine):
    at = lax.axis_index("dp")
    return place(at if mine else 1 - at, rows)


def conv_kernel(parts, *refs):
    conv = refs[:parts]
    spec_filt, fwd_hi, fwd_lo, inv_hi, inv_lo = refs[parts : parts + 5]
    out = refs[parts + 5 : 2 * parts + 5]
    spec_conv, whole = refs[2 * parts + 5 :]
    here = lax.axis_index("ctx")
    step = conv[1].shape[1]
    whole[:, place(here, step)] = conv[0][place(here, whole.shape[0]), :]
    for k, piece in zip(offsets(parts)[1:], conv[1:]):
        whole[:, place(here ^ k, step)] = piece[...]
    spec_conv[...] = spectrum_of(whole[...], fwd_hi, fwd_lo)
    product = spectrum_product(spec_filt[...], spec_conv[...], False)
    whole[...] = inverse_dense(product, inv_hi, inv_lo).astype(jnp.bfloat16)
    scatter_tokens(whole, out, here, range(parts))


def unit_rows(order, weight, gate, rows_all, unit, out):
    here = lax.axis_index("ctx")
    for k, grad, ref in zip(order, unit, out):
        rows = grad.shape[0]
        at = place(here ^ k, rows)
        got = mm_nt(weight[at, :], rows_all[...])
        grad[...] = got
        ref[...] = (got * gate[at, :].astype(jnp.float32)).astype(jnp.bfloat16)


def far_unit_kernel(order, pieces, after, weight, gate, *refs):
    grads, count = refs[:pieces], len(order)
    unit, out, rows_all = refs[pieces : pieces + count], refs[pieces + count : -1], refs[-1]
    block = lax.axis_index("tp")
    rows = grads[0].shape[0]
    cut = grads[3].shape[1]
    for k, ref in enumerate(grads[:3]):
        rows_all[place(block ^ k, rows), :] = ref[...]
    rows_all[place(block ^ 3, rows), :cut] = grads[3][...]
    rows_all[place(block ^ 3, rows), cut:] = grads[4][...]
    unit_rows(order, weight, gate, rows_all, unit, out)


def own_unit_kernel(order, weight, gate, rows_all, unit, out):
    unit_rows(order, weight, gate, rows_all, [unit], [out])


def grad_kernel(parts, *refs):
    gate = refs[:parts]
    spec_filt, fwd_hi, fwd_lo, inv_hi, inv_lo = refs[parts : parts + 5]
    out = refs[parts + 5 : 2 * parts + 5]
    spec_gate, whole = refs[2 * parts + 5 :]
    here = lax.axis_index("ctx")
    gather_tokens(gate, whole, here)
    spec_gate[...] = spectrum_of(whole[...], fwd_hi, fwd_lo)
    product = spectrum_product(spec_filt[...], spec_gate[...], True)
    whole[...] = inverse_dense(product, inv_hi, inv_lo).astype(jnp.bfloat16)
    scatter_tokens(whole, out, here, middle_offsets(parts))


def filter_kernel(parts, scale, spec_conv, spec_gate, inv_hi, inv_lo, *refs):
    keep, *send, whole = refs[1:]
    product = spectrum_product(spec_conv[...], spec_gate[...], True)
    whole[...] = inverse_dense(product, inv_hi, inv_lo) * scale
    rows = keep.shape[0]
    keep[...] = whole[pair_rows(rows, True), :]
    for i, ref in enumerate(send):
        step = ref.shape[0]
        at = pl.multiple_of(pair_rows(rows, False).start + i * step, step)
        ref[...] = whole[pl.ds(at, step), :].astype(jnp.bfloat16)


def gate_kernel(parts, *refs):
    unit, back, out = refs[:parts], refs[parts : 2 * parts], refs[2 * parts]
    here = lax.axis_index("ctx")
    rows = back[0].shape[0]
    for k, grad, ref in zip(range(parts), unit, back):
        gated = grad[...] * ref[...].astype(jnp.float32)
        out[place(here ^ k, rows), :] = gated.astype(jnp.bfloat16)


def last_kernel(parts, *refs):
    back, (low, high, keep, total, out) = refs[:parts], refs[parts:]
    step = low.shape[0]
    for i, ref in enumerate((low, high)):
        at = slice(i * step, (i + 1) * step)
        total[at, :] = keep[at, :] + ref[...].astype(jnp.float32)
    here = lax.axis_index("ctx")
    rows = back[0].shape[0]
    for k, ref in zip(middle_offsets(parts), back):
        out[place(here ^ k, rows), :] = ref[...]


def call(kernel, outs, args, scratch=(), far=(), cost=1.0):
    vmem = pl.BlockSpec(memory_space=pltpu.VMEM)
    hbm = pl.BlockSpec(memory_space=pltpu.HBM)
    held = [
        pltpu.with_memory_space_constraint(a, pltpu.HBM) if i in far else a
        for i, a in enumerate(args)
    ]
    return pl.pallas_call(
        kernel,
        out_shape=outs,
        in_specs=[hbm if i in far else vmem for i in range(len(args))],
        out_specs=jax.tree.map(lambda _: vmem, outs),
        scratch_shapes=list(scratch),
        cost_estimate=pl.CostEstimate(
            flops=int(cost * 1e9), bytes_accessed=int(cost * 1e6), transcendentals=0
        ),
        compiler_params=pltpu.CompilerParams(vmem_limit_bytes=VMEM_BYTES),
    )(*held)


def dense_on_device(parts, groups, out_grad, gate_in, conv_in, filter_raw, out_weight):
    f32, bf16 = jnp.float32, jnp.bfloat16
    grad_rows, gate_local, conv_local = out_grad[0], gate_in[0], conv_in[0]
    chans, length = filter_raw.shape
    channels, tokens = conv_local.shape
    width = grad_rows.shape[1]
    scale = 1.0 / math.sqrt(length)
    tables = [jnp.asarray(t) for t in dense_tables(length)]
    shape = jax.ShapeDtypeStruct

    def swap(value, axis, size, k):
        return lax.ppermute(value, axis, [(i, i ^ k) for i in range(size)])

    def exchange(pieces, order):
        return [swap(p, "ctx", parts, k) if k else p for k, p in zip(order, pieces)]

    grad_1 = swap(grad_rows, "tp", groups, 1)
    grad_2 = swap(grad_rows, "tp", groups, 2)
    blocks = call(
        blocks_kernel,
        [shape((chans, tokens), bf16)] * (parts - 1),
        [conv_local],
        [pltpu.SemaphoreType.DMA((parts - 1,))],
        far=(0,),
        cost=10.0,
    )
    conv_pieces = exchange(blocks, offsets(parts)[1:])
    cut = width // 32 * 11
    grad_3a = swap(grad_1[:, :cut], "tp", groups, 2)
    grad_3b = swap(grad_2[:, cut:], "tp", groups, 1)

    piece = shape((chans, tokens), bf16)
    spectrum = shape((chans, 2 * length), f32)
    whole = pltpu.VMEM((chans, length), bf16)
    spec_filt = call(
        functools.partial(filt_kernel, scale),
        spectrum,
        [filter_raw, *tables[:2], grad_1, grad_2],
        cost=2.0,
    )
    *conv_out, spec_conv = call(
        functools.partial(conv_kernel, parts),
        [piece] * parts + [spectrum],
        [conv_local, *conv_pieces, spec_filt, *tables],
        [whole],
        cost=2.0,
    )

    away = offsets(parts)[1:]
    grad_all = shape((groups * grad_rows.shape[0], width), bf16)
    unit_piece = shape((chans, tokens), f32)
    *far, grad_all = call(
        functools.partial(far_unit_kernel, away, 5),
        [unit_piece] * len(away) + [piece] * len(away) + [grad_all],
        [conv_out[0], out_weight, gate_local, grad_rows, grad_1, grad_2, grad_3a, grad_3b],
    )
    unit_own, gate_own = call(
        functools.partial(own_unit_kernel, [0]),
        [unit_piece, piece],
        [out_weight, gate_local, grad_all],
    )
    *conv_out, gate_own = lax.optimization_barrier((*conv_out, gate_own))
    conv_back = exchange(conv_out, range(parts))
    gate_chan = exchange([gate_own, *far[len(away) :]], offsets(parts))
    unit = dict(zip(offsets(parts), [unit_own, *far[: len(away)]]))
    *conv_grad, spec_gate = call(
        functools.partial(grad_kernel, parts),
        [piece] * parts + [spectrum],
        [*gate_chan, spec_filt, *tables],
        [whole],
    )
    grad_back = exchange(conv_grad, middle_offsets(parts))
    half, local = shape((chans // 2, length), f32), shape((channels, tokens), bf16)
    quarter = shape((chans // 4, length), bf16)
    gate_out = call(
        functools.partial(gate_kernel, parts),
        local,
        [*(unit[k] for k in range(parts)), *conv_back],
    )
    keep, send_low, send_high = call(
        functools.partial(filter_kernel, parts, scale),
        [half, quarter, quarter],
        [spec_conv, spec_gate, *tables[2:], conv_back[1]],
        [pltpu.VMEM((chans, length), f32)],
        cost=2.0,
    )
    filter_grad, conv_grad_out = call(
        functools.partial(last_kernel, parts),
        [half, local],
        [*grad_back, swap(send_low, "dp", 2, 1), swap(send_high, "dp", 2, 1), keep],
    )
    return (gate_out[None], conv_grad_out[None], filter_grad)


def solution(mesh):
    placed = (
        P("dp", ("ctx", "tp"), None),
        P("dp", "tp", "ctx"),
        P("dp", "tp", "ctx"),
        P(("tp", "ctx"), None),
        P("tp", None),
    )
    parts, groups, pair = mesh.shape["ctx"], mesh.shape["tp"], mesh.shape["dp"]

    def on_device(out_grad, gate_in, conv_in, filter_raw, out_weight):
        args = (out_grad, gate_in, conv_in, filter_raw, out_weight)
        table = 4 * filter_raw.shape[1] ** 2 * jnp.dtype(jnp.bfloat16).itemsize
        one_sequence = out_grad.shape[0] == 1
        power = parts & (parts - 1) == 0
        if one_sequence and power and parts > 1 and groups == 4 and pair == 2 and table <= TABLE_LIMIT_BYTES:
            return dense_on_device(parts, groups, *args)
        return two_level_on_device(*args)

    return jax.shard_map(
        on_device,
        mesh=mesh,
        in_specs=placed,
        out_specs=(P("dp", "tp", "ctx"), P("dp", "tp", "ctx"), P(("tp", "ctx", "dp"), None)),
        check_vma=False,
    )
```

```python
import functools
import math

import jax
import jax.numpy as jnp
import ml_dtypes
import numpy as np
from jax import lax
from jax.experimental import pallas as pl
from jax.experimental.pallas import tpu as pltpu
from jax.sharding import PartitionSpec as P


def wave_table(rows, cols, length, sign):
    product = (
        jnp.arange(rows, dtype=jnp.int32)[:, None]
        * jnp.arange(cols, dtype=jnp.int32)[None, :]
        % length
    )
    angle = product.astype(jnp.float32) * (2.0 * math.pi / length)
    return (jnp.cos(angle), sign * jnp.sin(angle))


def mix_einsum(form, left, right):
    return jnp.einsum(form, left, right, precision=lax.Precision.HIGHEST)


def forward_spectrum(signal):
    chans, length = signal.shape
    total_len = 2 * length
    bits = total_len.bit_length() - 1
    outer_len = 2 ** (bits // 2)
    inner_len = total_len // outer_len
    half_outer = outer_len // 2
    folded = signal.reshape(chans, half_outer, inner_len)
    first_re, first_im = wave_table(outer_len, half_outer, outer_len, -1.0)
    mid_re = mix_einsum("kn,cna->cka", first_re, folded)
    mid_im = mix_einsum("kn,cna->cka", first_im, folded)
    twist_re, twist_im = wave_table(outer_len, inner_len, total_len, -1.0)
    rot_re = mid_re * twist_re - mid_im * twist_im
    rot_im = mid_re * twist_im + mid_im * twist_re
    last_re, last_im = wave_table(inner_len, inner_len, inner_len, -1.0)
    out_re = mix_einsum("cka,aj->ckj", rot_re, last_re) - mix_einsum("cka,aj->ckj", rot_im, last_im)
    out_im = mix_einsum("cka,aj->ckj", rot_re, last_im) + mix_einsum("cka,aj->ckj", rot_im, last_re)
    return (out_re, out_im)


def inverse_signal(spec_re, spec_im):
    chans, outer_len, inner_len = spec_re.shape
    total_len = outer_len * inner_len
    last_re, last_im = wave_table(inner_len, inner_len, inner_len, 1.0)
    mid_re = mix_einsum("ckj,ja->cka", spec_re, last_re) - mix_einsum(
        "ckj,ja->cka", spec_im, last_im
    )
    mid_im = mix_einsum("ckj,ja->cka", spec_re, last_im) + mix_einsum(
        "ckj,ja->cka", spec_im, last_re
    )
    twist_re, twist_im = wave_table(outer_len, inner_len, total_len, 1.0)
    rot_re = mid_re * twist_re - mid_im * twist_im
    rot_im = mid_re * twist_im + mid_im * twist_re
    first_re, first_im = wave_table(outer_len // 2, outer_len, outer_len, 1.0)
    signal = mix_einsum("nk,cka->cna", first_re, rot_re) - mix_einsum(
        "nk,cka->cna", first_im, rot_im
    )
    return signal.reshape(chans, -1) / total_len


def two_level_on_device(out_grad, gate_in, conv_in, filter_raw, out_weight):
    grad_rows = out_grad[0]
    gate_local = gate_in[0]
    conv_local = conv_in[0]
    unit_grad = lax.dot_general(
        out_weight,
        lax.all_gather(grad_rows, "tp", axis=0, tiled=True),
        (((1,), (1,)), ((), ())),
        preferred_element_type=jnp.float32,
    )
    gate_grad = (unit_grad * gate_local.astype(jnp.float32)).astype(jnp.bfloat16)
    gate_chan, conv_chan = (
        lax.all_to_all(gate_grad, "ctx", split_axis=0, concat_axis=1, tiled=True),
        lax.all_to_all(conv_local, "ctx", split_axis=0, concat_axis=1, tiled=True),
    )
    length = filter_raw.shape[1]
    norm_scale = 1.0 / math.sqrt(length)
    filt_re, filt_im = forward_spectrum(filter_raw * norm_scale)
    conv_re, conv_im = forward_spectrum(conv_chan.astype(jnp.float32))
    gate_re, gate_im = forward_spectrum(gate_chan.astype(jnp.float32))
    conv_out = inverse_signal(
        filt_re * conv_re - filt_im * conv_im, filt_re * conv_im + filt_im * conv_re
    ).astype(jnp.bfloat16)
    conv_grad = inverse_signal(
        filt_re * gate_re + filt_im * gate_im, filt_re * gate_im - filt_im * gate_re
    ).astype(jnp.bfloat16)
    cross_re = gate_re * conv_re + gate_im * conv_im
    cross_im = gate_im * conv_re - gate_re * conv_im
    back_out, back_grad = (
        lax.all_to_all(conv_out, "ctx", split_axis=1, concat_axis=0, tiled=True),
        lax.all_to_all(conv_grad, "ctx", split_axis=1, concat_axis=0, tiled=True),
    )
    gate_out = (unit_grad * back_out.astype(jnp.float32)).astype(jnp.bfloat16)
    summed_re, summed_im = (
        lax.psum_scatter(cross_re * norm_scale, "dp", scatter_dimension=0, tiled=True),
        lax.psum_scatter(cross_im * norm_scale, "dp", scatter_dimension=0, tiled=True),
    )
    filter_grad = inverse_signal(summed_re, summed_im)
    return (gate_out[None], back_grad[None], filter_grad)


TABLE_LIMIT_BYTES = 4 * 2**20
VMEM_BYTES = 24 * 2**20


def split_high_low(values):
    high = values.astype(ml_dtypes.bfloat16)
    low = (values - high.astype(np.float64)).astype(ml_dtypes.bfloat16)
    return high, low


@functools.lru_cache(maxsize=None)
def dense_tables(length):
    total = 2 * length
    time = np.arange(length)[:, None]
    freq = np.arange(length)[None, :]
    angle = (time * freq % total) * (2.0 * np.pi / total)
    even_odd = 1.0 - 2.0 * (np.arange(length) % 2)
    real, imag = np.cos(angle), -np.sin(angle)
    imag[:, 0] = even_odd
    weight = np.full((length, 1), 2.0 / total)
    weight[0] = 1.0 / total
    forward = np.concatenate([real, imag], axis=1)
    inverse = np.concatenate([real.T * weight, imag.T * weight], axis=0)
    return split_high_low(forward) + split_high_low(inverse)


def mm(left, right):
    return jnp.dot(left, right, preferred_element_type=jnp.float32)


def mm_nt(left, right):
    return lax.dot_general(left, right, (((1,), (1,)), ((), ())), preferred_element_type=jnp.float32)


def halves(values):
    high = values.astype(jnp.bfloat16)
    return high, (values - high.astype(jnp.float32)).astype(jnp.bfloat16)


def spectrum_product(left, right, conj_left):
    length = left.shape[1] // 2
    lr, li = left[:, :length], left[:, length:]
    rr, ri = right[:, :length], right[:, length:]
    ends = lax.broadcasted_iota(jnp.int32, lr.shape, 1) == 0
    both = li * ri
    if conj_left:
        real = lr * rr + jnp.where(ends, 0.0, both)
        imag = jnp.where(ends, both, lr * ri - li * rr)
    else:
        real = lr * rr - jnp.where(ends, 0.0, both)
        imag = jnp.where(ends, both, lr * ri + li * rr)
    return jnp.concatenate([real, imag], axis=1)


def inverse_dense(spec, inv_hi, inv_lo):
    high, low = halves(spec)
    return mm(high, inv_hi[...]) + mm(high, inv_lo[...]) + mm(low, inv_hi[...])


def place(index, size):
    return pl.ds(pl.multiple_of(index * size, size), size)


def offsets(parts):
    return [0, *reversed(range(1, parts))]


def middle_offsets(parts):
    return [0, *range(parts // 2, parts), *range(1, parts // 2)]


def gather_tokens(pieces, whole, here):
    step = pieces[0].shape[1]
    for k, piece in zip(offsets(len(pieces)), pieces):
        whole[:, place(here ^ k, step)] = piece[...]


def scatter_tokens(whole, pieces, here, order):
    step = pieces[0].shape[1]
    for k, piece in zip(order, pieces):
        piece[...] = whole[:, place(here ^ k, step)]


def blocks_kernel(source, *refs):
    out, sems = refs[:-1], refs[-1]
    here = lax.axis_index("ctx")
    rows = out[0].shape[0]
    copies = [
        pltpu.make_async_copy(source.at[place(here ^ k, rows), :], ref, sems.at[k - 1])
        for k, ref in zip(offsets(len(out) + 1)[1:], out)
    ]
    for copy in copies:
        copy.start()
    for copy in copies:
        copy.wait()


def filt_kernel(scale, filt, fwd_hi, fwd_lo, after_1, after_2, spec_filt):
    high, low = halves(filt[...] * scale)
    spec_filt[...] = mm(high, fwd_hi[...]) + mm(low, fwd_hi[...]) + mm(high, fwd_lo[...])


def spectrum_of(signal, fwd_hi, fwd_lo):
    return mm(signal, fwd_hi[...]) + mm(signal, fwd_lo[...])


def pair_rows(rows, mine):
    at = lax.axis_index("dp")
    return place(at if mine else 1 - at, rows)


def conv_kernel(parts, *refs):
    conv = refs[:parts]
    spec_filt, fwd_hi, fwd_lo, inv_hi, inv_lo = refs[parts : parts + 5]
    out = refs[parts + 5 : 2 * parts + 5]
    spec_conv, whole = refs[2 * parts + 5 :]
    here = lax.axis_index("ctx")
    step = conv[1].shape[1]
    whole[:, place(here, step)] = conv[0][place(here, whole.shape[0]), :]
    for k, piece in zip(offsets(parts)[1:], conv[1:]):
        whole[:, place(here ^ k, step)] = piece[...]
    spec_conv[...] = spectrum_of(whole[...], fwd_hi, fwd_lo)
    product = spectrum_product(spec_filt[...], spec_conv[...], False)
    whole[...] = inverse_dense(product, inv_hi, inv_lo).astype(jnp.bfloat16)
    scatter_tokens(whole, out, here, range(parts))


def unit_rows(order, weight, gate, rows_all, unit, out):
    here = lax.axis_index("ctx")
    for k, grad, ref in zip(order, unit, out):
        rows = grad.shape[0]
        at = place(here ^ k, rows)
        got = mm_nt(weight[at, :], rows_all[...])
        grad[...] = got
        ref[...] = (got * gate[at, :].astype(jnp.float32)).astype(jnp.bfloat16)


def far_unit_kernel(order, pieces, after, weight, gate, *refs):
    grads, count = refs[:pieces], len(order)
    unit, out, rows_all = refs[pieces : pieces + count], refs[pieces + count : -1], refs[-1]
    block = lax.axis_index("tp")
    rows = grads[0].shape[0]
    cut = grads[3].shape[1]
    for k, ref in enumerate(grads[:3]):
        rows_all[place(block ^ k, rows), :] = ref[...]
    rows_all[place(block ^ 3, rows), :cut] = grads[3][...]
    rows_all[place(block ^ 3, rows), cut:] = grads[4][...]
    unit_rows(order, weight, gate, rows_all, unit, out)


def own_unit_kernel(order, weight, gate, rows_all, unit, out):
    unit_rows(order, weight, gate, rows_all, [unit], [out])


def grad_kernel(parts, *refs):
    gate = refs[:parts]
    spec_filt, fwd_hi, fwd_lo, inv_hi, inv_lo = refs[parts : parts + 5]
    out = refs[parts + 5 : 2 * parts + 5]
    spec_gate, whole = refs[2 * parts + 5 :]
    here = lax.axis_index("ctx")
    gather_tokens(gate, whole, here)
    spec_gate[...] = spectrum_of(whole[...], fwd_hi, fwd_lo)
    product = spectrum_product(spec_filt[...], spec_gate[...], True)
    whole[...] = inverse_dense(product, inv_hi, inv_lo).astype(jnp.bfloat16)
    scatter_tokens(whole, out, here, middle_offsets(parts))


def filter_kernel(parts, scale, spec_conv, spec_gate, inv_hi, inv_lo, *refs):
    keep, *send, whole = refs[parts - 2 :]
    product = spectrum_product(spec_conv[...], spec_gate[...], True)
    whole[...] = inverse_dense(product, inv_hi, inv_lo) * scale
    rows = keep.shape[0]
    keep[...] = whole[pair_rows(rows, True), :]
    for i, ref in enumerate(send):
        step = ref.shape[0]
        at = pl.multiple_of(pair_rows(rows, False).start + i * step, step)
        ref[...] = whole[pl.ds(at, step), :].astype(jnp.bfloat16)


def gate_kernel(parts, *refs):
    unit, back, out = refs[:parts], refs[parts : 2 * parts], refs[2 * parts]
    here = lax.axis_index("ctx")
    rows = back[0].shape[0]
    for k, grad, ref in zip(range(parts), unit, back):
        gated = grad[...] * ref[...].astype(jnp.float32)
        out[place(here ^ k, rows), :] = gated.astype(jnp.bfloat16)


def last_kernel(parts, *refs):
    back, (low, high, keep, total, out) = refs[:parts], refs[parts:]
    step = low.shape[0]
    for i, ref in enumerate((low, high)):
        at = slice(i * step, (i + 1) * step)
        total[at, :] = keep[at, :] + ref[...].astype(jnp.float32)
    here = lax.axis_index("ctx")
    rows = back[0].shape[0]
    for k, ref in zip(middle_offsets(parts), back):
        out[place(here ^ k, rows), :] = ref[...]


def call(kernel, outs, args, scratch=(), far=(), cost=1.0):
    vmem = pl.BlockSpec(memory_space=pltpu.VMEM)
    hbm = pl.BlockSpec(memory_space=pltpu.HBM)
    held = [
        pltpu.with_memory_space_constraint(a, pltpu.HBM) if i in far else a
        for i, a in enumerate(args)
    ]
    return pl.pallas_call(
        kernel,
        out_shape=outs,
        in_specs=[hbm if i in far else vmem for i in range(len(args))],
        out_specs=jax.tree.map(lambda _: vmem, outs),
        scratch_shapes=list(scratch),
        cost_estimate=pl.CostEstimate(
            flops=int(cost * 1e9), bytes_accessed=int(cost * 1e6), transcendentals=0
        ),
        compiler_params=pltpu.CompilerParams(vmem_limit_bytes=VMEM_BYTES),
    )(*held)


def dense_on_device(parts, groups, out_grad, gate_in, conv_in, filter_raw, out_weight):
    f32, bf16 = jnp.float32, jnp.bfloat16
    grad_rows, gate_local, conv_local = out_grad[0], gate_in[0], conv_in[0]
    chans, length = filter_raw.shape
    channels, tokens = conv_local.shape
    width = grad_rows.shape[1]
    scale = 1.0 / math.sqrt(length)
    tables = [jnp.asarray(t) for t in dense_tables(length)]
    shape = jax.ShapeDtypeStruct

    def swap(value, axis, size, k):
        return lax.ppermute(value, axis, [(i, i ^ k) for i in range(size)])

    def exchange(pieces, order):
        return [swap(p, "ctx", parts, k) if k else p for k, p in zip(order, pieces)]

    grad_1 = swap(grad_rows, "tp", groups, 1)
    grad_2 = swap(grad_rows, "tp", groups, 2)
    blocks = call(
        blocks_kernel,
        [shape((chans, tokens), bf16)] * (parts - 1),
        [conv_local],
        [pltpu.SemaphoreType.DMA((parts - 1,))],
        far=(0,),
        cost=10.0,
    )
    conv_pieces = exchange(blocks, offsets(parts)[1:])
    cut = width // 32 * 11
    grad_3a = swap(grad_1[:, :cut], "tp", groups, 2)
    grad_3b = swap(grad_2[:, cut:], "tp", groups, 1)

    piece = shape((chans, tokens), bf16)
    spectrum = shape((chans, 2 * length), f32)
    whole = pltpu.VMEM((chans, length), bf16)
    spec_filt = call(
        functools.partial(filt_kernel, scale),
        spectrum,
        [filter_raw, *tables[:2], grad_1, grad_2],
        cost=2.0,
    )
    *conv_out, spec_conv = call(
        functools.partial(conv_kernel, parts),
        [piece] * parts + [spectrum],
        [conv_local, *conv_pieces, spec_filt, *tables],
        [whole],
        cost=2.0,
    )

    away = offsets(parts)[1:]
    grad_all = shape((groups * grad_rows.shape[0], width), bf16)
    unit_piece = shape((chans, tokens), f32)
    *far, grad_all = call(
        functools.partial(far_unit_kernel, away, 5),
        [unit_piece] * len(away) + [piece] * len(away) + [grad_all],
        [conv_out[0], out_weight, gate_local, grad_rows, grad_1, grad_2, grad_3a, grad_3b],
    )
    unit_own, gate_own = call(
        functools.partial(own_unit_kernel, [0]),
        [unit_piece, piece],
        [out_weight, gate_local, grad_all],
    )
    *conv_out, gate_own = lax.optimization_barrier((*conv_out, gate_own))
    conv_back = exchange(conv_out, range(parts))
    gate_chan = exchange([gate_own, *far[len(away) :]], offsets(parts))
    unit = dict(zip(offsets(parts), [unit_own, *far[: len(away)]]))
    *conv_grad, spec_gate = call(
        functools.partial(grad_kernel, parts),
        [piece] * parts + [spectrum],
        [*gate_chan, spec_filt, *tables],
        [whole],
    )
    grad_back = exchange(conv_grad, middle_offsets(parts))
    half, local = shape((chans // 2, length), f32), shape((channels, tokens), bf16)
    quarter = shape((chans // 4, length), bf16)
    gate_out = call(
        functools.partial(gate_kernel, parts),
        local,
        [*(unit[k] for k in range(parts)), *conv_back],
    )
    keep, send_low, send_high = call(
        functools.partial(filter_kernel, parts, scale),
        [half, quarter, quarter],
        [spec_conv, spec_gate, *tables[2:], *conv_back[1:-1]],
        [pltpu.VMEM((chans, length), f32)],
        cost=2.0,
    )
    filter_grad, conv_grad_out = call(
        functools.partial(last_kernel, parts),
        [half, local],
        [*grad_back, swap(send_low, "dp", 2, 1), swap(send_high, "dp", 2, 1), keep],
    )
    return (gate_out[None], conv_grad_out[None], filter_grad)


def solution(mesh):
    placed = (
        P("dp", ("ctx", "tp"), None),
        P("dp", "tp", "ctx"),
        P("dp", "tp", "ctx"),
        P(("tp", "ctx"), None),
        P("tp", None),
    )
    parts, groups, pair = mesh.shape["ctx"], mesh.shape["tp"], mesh.shape["dp"]

    def on_device(out_grad, gate_in, conv_in, filter_raw, out_weight):
        args = (out_grad, gate_in, conv_in, filter_raw, out_weight)
        table = 4 * filter_raw.shape[1] ** 2 * jnp.dtype(jnp.bfloat16).itemsize
        one_sequence = out_grad.shape[0] == 1
        power = parts & (parts - 1) == 0
        if one_sequence and power and parts > 1 and groups == 4 and pair == 2 and table <= TABLE_LIMIT_BYTES:
            return dense_on_device(parts, groups, *args)
        return two_level_on_device(*args)

    return jax.shard_map(
        on_device,
        mesh=mesh,
        in_specs=placed,
        out_specs=(P("dp", "tp", "ctx"), P("dp", "tp", "ctx"), P(("tp", "ctx", "dp"), None)),
        check_vma=False,
    )
```
